256 devices in a mesh: lat: 16 (over x_lo, y, core), lon: 16 (over x_hi, z).
Axes of the slice: x: 4 (x_hi: 2, x_lo: 2; x = x_hi * 2 + x_lo), y: 4, z: 8, core: 2. Of those that a mesh axis runs over, the one named last changes fastest.
Arguments:
- state: float32 [512, 3600, 128], P('lat', 'lon'), may hold values from -6 to 6
- zonal_coef: float32 [512], P('lat'), may hold values from 0.02 to 0.2
- diffusivity: float32 [128], replicated, may hold values from 0.5 to 2
- coupling: float32 [128, 128], replicated, may hold values from -0.5 to 0.5
- filter_rows: int32 [192], replicated, may hold values from 0 to 511, as said below
- band_width: int32 [512], replicated, may hold values from 1 to 16
- table_index: int32 [512], replicated, may hold values from 0 to 15
- coef_table: float32 [16, 17], replicated, may hold values from -1.2 to 1.2
Outputs:
- updated: float32 [512, 3600, 128], P('lat', 'lon')
The draws below stay inside these ranges and needn't reach their ends.
Inputs may be any that keep to these rules, and one draw needn't show every extreme that they name: `filter_rows`: 192 distinct rows in increasing order: every row less than 64 rows from either pole, and half of the rows from 64 to 128 rows from each pole.
All inputs are finite; a program needn't handle non-finite values.
Results may differ from the reference program's by a relative error of at most 0.00007.
Values sent between devices are 32-bit elements; how exact they have to be, the bound alone decides.
A program may use at most 128 MiB of HBM per device.

```python
import math
import jax
import jax.numpy as jnp
from jax import lax

NLON = 3600
MAXB = 16
NTAB = 16
CH = 128
NLAT = 512


def draw_filter_rows(key, part):
    key = jax.random.fold_in(key, 11)
    north_key, south_key = jax.random.split(key)
    eighth = NLAT // 8
    sixteenth = NLAT // 16
    north_pick = jnp.sort(jax.random.permutation(north_key, eighth)[:sixteenth]) + eighth
    south_pick = jnp.sort(jax.random.permutation(south_key, eighth)[:sixteenth]) + NLAT - 2 * eighth
    return jnp.concatenate([jnp.arange(eighth), north_pick, south_pick, jnp.arange(NLAT - eighth, NLAT)]).astype(jnp.int32)


def draw_band_width(key, part):
    key = jax.random.fold_in(key, 23)
    width_key, place_key = jax.random.split(key)
    widths = jax.random.randint(width_key, (NLAT,), 1, MAXB + 1)
    place = jax.random.randint(place_key, (), 0, NLAT // 8)
    return widths.at[place].set(MAXB).astype(jnp.int32)


def place_ends(drawn, key, smallest, high):
    longest = drawn.shape.index(max(drawn.shape))
    spots = []
    for shift in (0, 1):
        where = [jax.random.randint(jax.random.fold_in(key, axis), (), 0, length) for axis, length in enumerate(drawn.shape)]
        where[longest] = (where[longest] + shift) % drawn.shape[longest]
        spots.append(tuple(where))
    return drawn.at[spots[0]].set(smallest).at[spots[1]].set(high)


def shard_levels(stream_key, shape, pieces, smallest, high):
    def one(dim, shards_of):
        steps = jax.random.uniform(jax.random.fold_in(jax.random.fold_in(stream_key, 6), dim), (shards_of,), jnp.float32, smallest / len(pieces), high / len(pieces))
        return jnp.repeat(jnp.exp(steps), shape[dim] // shards_of).reshape((-1,) + (1,) * (len(shape) - dim - 1))

    factor_of = one(*pieces[0])
    for cut in pieces[1:]:
        factor_of = factor_of * one(*cut)
    return factor_of


def centred(key, dims, width, most, pieces=(), dtype=jnp.bfloat16):
    gain = shard_levels(key, dims, pieces, -0.22, 0.18) if pieces else 1.0
    drawn = jax.random.normal(key, dims, jnp.float32) * width * gain
    return jnp.minimum(jnp.maximum(drawn, -most), most).astype(dtype)


def setup_inputs(seed: int = 0) -> dict:
    splits = jax.random.split(jax.random.key(seed), 9)
    return {
        "state": centred(splits[0], (NLAT, NLON, CH), 1.0, 6.0, ((0, 16), (1, 16)), jnp.float32),
        "zonal_coef": jnp.clip(jnp.exp(math.log(0.2) - 2.3025851 * jax.random.uniform(splits[1], (NLAT,), jnp.float32) ** shard_levels(splits[1], (NLAT,), ((0, 16),), -0.2, 0.2)), 0.02, 0.2),
        "diffusivity": jnp.clip(jnp.exp(jax.random.uniform(splits[2], (CH,), jnp.float32, math.log(0.5), math.log(2.0))), 0.5, 2.0),
        "coupling": centred(splits[3], (CH, CH), CH ** -0.5, 0.5, (), jnp.float32),
        "filter_rows": draw_filter_rows(jax.random.fold_in(splits[8], 71), 0),
        "band_width": draw_band_width(jax.random.fold_in(splits[8], 71), 0),
        "table_index": place_ends(jax.random.randint(splits[6], (NLAT,), 0, NTAB), jax.random.fold_in(splits[6], 1), 0, NTAB - 1).astype(jnp.int32),
        "coef_table": centred(splits[7], (NTAB, MAXB + 1), 0.2, 1.2, (), jnp.float32),
    }


meridional_rate = 0.1


def row_weights(rows, band_width, table_index, coef_table):
    tables = table_index[rows]
    choose = (tables[:, None] == jnp.arange(coef_table.shape[0])[None, :]).astype(jnp.float32)
    picked = jnp.dot(choose, coef_table, precision=lax.Precision.HIGHEST, preferred_element_type=jnp.float32)
    reach = jnp.arange(coef_table.shape[1])[None, :] <= band_width[rows][:, None]
    return jnp.where(reach, picked, jnp.float32(0.0))


def reference(state, zonal_coef, diffusivity, coupling, filter_rows, band_width, table_index, coef_table):
    padded = jnp.pad(state, ((1, 1), (0, 0), (0, 0)))
    east = jnp.roll(state, -1, axis=1)
    west = jnp.roll(state, 1, axis=1)
    north = padded[2:]
    south = padded[:-2]
    tendency = zonal_coef[:, None, None] * (east + west - 2.0 * state) + meridional_rate * (north + south - 2.0 * state)
    stepped = state + diffusivity[None, None, :] * tendency
    flat = stepped.reshape(-1, stepped.shape[2])
    coupled = stepped + jnp.dot(flat, coupling, precision=lax.Precision.HIGHEST, preferred_element_type=jnp.float32).reshape(stepped.shape)
    weights = row_weights(filter_rows, band_width, table_index, coef_table)
    picked = coupled[filter_rows]
    total = weights[:, 0, None, None] * picked
    for step in range(1, MAXB + 1):
        total = total + weights[:, step, None, None] * (jnp.roll(picked, step, axis=1) + jnp.roll(picked, -step, axis=1))
    return coupled.at[filter_rows].set(total)
```

```python
import jax
import jax.numpy as jnp
from jax import lax
from jax.experimental import pallas as pl
from jax.experimental.pallas import tpu as pltpu
from jax.sharding import PartitionSpec as P

MAXB = 16
HALO = MAXB + 1
MERIDIONAL = 0.1
ROWS = 32
COLS = 225
CH = 128
TILES = ROWS // 8
CHUNK = 32
BLOCK = 8
MESH = pl.DeviceIdType.MESH
F32 = jnp.float32
BF16 = jnp.bfloat16


def chunks(total, size):
    return [min(i * size, total - size) for i in range((total + size - 1) // size)]


def kernel(
    st, zc, df, cp, fr, bw, ti, ct, out,
    S, C, W, A, C0, R, zc_v, df_v, cp_v, fr_v, bw_v, ti_v, ct_v, ss, rs, ls,
):
    la = lax.axis_index("lat")
    lo = lax.axis_index("lon")
    east = lax.rem(lo + 1, 16)
    west = lax.rem(lo + 15, 16)

    def is_polar(pos):
        return (pos < 4) | (pos >= 12)

    polar = is_polar(la)
    has_up = la < 15
    has_down = la > 0
    corner_up = has_up & (polar | is_polar(la + 1))
    corner_down = has_down & (polar | is_polar(la - 1))

    barrier = pltpu.get_barrier_semaphore()

    def greet(*who):
        for device in who:
            pl.semaphore_signal(barrier, inc=1, device_id=device, device_id_type=MESH)

    greet((la, east), (la, west))
    pl.when(has_up)(lambda: greet((la + 1, lo)))
    pl.when(has_down)(lambda: greet((la - 1, lo)))
    pl.when(corner_up)(lambda: greet((la + 1, east), (la + 1, west)))
    pl.when(corner_down)(lambda: greet((la - 1, east), (la - 1, west)))

    small = [(zc, zc_v), (df, df_v), (cp, cp_v), (fr, fr_v), (bw, bw_v), (ti, ti_v), (ct, ct_v)]
    loads = [pltpu.make_async_copy(src, dst, ls.at[i]) for i, (src, dst) in enumerate(small)]
    body = pltpu.make_async_copy(st, S.at[HALO : HALO + COLS, 8 : 8 + ROWS], ls.at[7])
    body.start()
    for load in loads:
        load.start()

    count = (
        2
        + jnp.where(has_up, 1, 0)
        + jnp.where(has_down, 1, 0)
        + jnp.where(corner_up, 2, 0)
        + jnp.where(corner_down, 2, 0)
    )
    pl.semaphore_wait(barrier, count)

    def send(src, dst, i, device):
        return pltpu.make_async_remote_copy(
            src_ref=src, dst_ref=dst, send_sem=ss.at[i], recv_sem=rs.at[i],
            device_id=device, device_id_type=MESH,
        )

    last = COLS - HALO
    high = HALO + COLS
    wide = []
    for t in range(TILES):
        here, there = slice(8 * t, 8 * t + 8), slice(8 * t + 8, 8 * t + 16)
        wide.append(
            (
                send(st.at[last:COLS, here], S.at[0:HALO, there], 2 * t, (la, east)),
                send(st.at[0:HALO, here], S.at[high : high + HALO, there], 2 * t + 1, (la, west)),
            )
        )
    thin = (
        send(st.at[COLS - 1 : COLS], S.at[HALO - 1 : HALO, 8 : 8 + ROWS], 0, (la, east)),
        send(st.at[0:1], S.at[high : high + 1, 8 : 8 + ROWS], 1, (la, west)),
    )
    up = send(st.at[:, 31:32], S.at[HALO:high, 7:8], 8, (la + 1, lo))
    down = send(st.at[:, 0:1], S.at[HALO:high, 40:41], 9, (la - 1, lo))
    up_east = send(st.at[last:COLS, 31:32], S.at[0:HALO, 7:8], 10, (la + 1, east))
    up_west = send(st.at[0:HALO, 31:32], S.at[high : high + HALO, 7:8], 11, (la + 1, west))
    down_east = send(st.at[last:COLS, 0:1], S.at[0:HALO, 40:41], 12, (la - 1, east))
    down_west = send(st.at[0:HALO, 0:1], S.at[high : high + HALO, 40:41], 13, (la - 1, west))

    def start(*copies):
        for copy in copies:
            copy.start()

    def wait_send(*copies):
        for copy in copies:
            copy.wait_send()

    def wait_recv(*copies):
        for copy in copies:
            copy.wait_recv()

    pl.when(polar)(lambda: start(*[copy for pair in wide for copy in pair]))
    pl.when(jnp.logical_not(polar))(lambda: start(*thin))
    pl.when(has_up)(lambda: start(up))
    pl.when(has_down)(lambda: start(down))
    to_up = has_up & is_polar(la + 1)
    to_down = has_down & is_polar(la - 1)
    pl.when(to_up)(lambda: start(up_east, up_west))
    pl.when(to_down)(lambda: start(down_east, down_west))

    def clear(row):
        S[:, row : row + 1, :] = jnp.zeros((S.shape[0], 1, CH), F32)

    pl.when(jnp.logical_not(has_down))(lambda: clear(7))
    pl.when(jnp.logical_not(has_up))(lambda: clear(40))

    for load in loads:
        load.wait()

    def iota(shape, dim):
        return lax.broadcasted_iota(jnp.int32, shape, dim)

    def column(values, offset):
        width = values.shape[1]
        pick = iota((ROWS, width), 1) == iota((ROWS, width), 0) + offset
        return jnp.sum(jnp.where(pick, values.astype(F32), 0.0), axis=1, keepdims=True)

    zonal = column(zc_v[...], 0)
    spread = df_v[...]
    A[...] = zonal * spread
    C0[...] = 1.0 - 2.0 * (zonal + MERIDIONAL) * spread
    fine = cp_v[...]
    coarse = fine.astype(BF16)
    rest = (fine - coarse.astype(F32)).astype(BF16)
    both = jnp.concatenate([coarse, rest], axis=1)
    R[...] = jnp.concatenate([both, both], axis=0)

    @pl.when(polar)
    def _():
        first = la * ROWS
        tables = column(ti_v[...], first)
        widths = column(bw_v[...], first)
        same = fr_v[...] == iota((ROWS, fr_v.shape[1]), 0) + first
        listed = jnp.sum(jnp.where(same, 1.0, 0.0), axis=1, keepdims=True) > 0.5
        taps = ct_v.shape[1]
        picked = jnp.zeros((ROWS, taps), F32)
        for table in range(ct_v.shape[0]):
            picked = jnp.where(tables == float(table), ct_v[table : table + 1, :], picked)
        reach = iota((ROWS, taps), 1)
        picked = jnp.where(reach.astype(F32) <= widths, picked, 0.0)
        picked = jnp.where(listed, picked, jnp.where(reach == 0, 1.0, 0.0))
        for k in range(taps):
            W[k] = jnp.broadcast_to(picked[:, k : k + 1], (ROWS, CH)).reshape(TILES, 8, CH)

    def couple(t, q0, size):
        low = 8 + 8 * t
        centre = S[pl.ds(q0 + 1, size), low : low + 8, :]
        sides = S[pl.ds(q0 + 2, size), low : low + 8, :] + S[pl.ds(q0, size), low : low + 8, :]
        poles = (
            S[pl.ds(q0 + 1, size), low + 1 : low + 9, :]
            + S[pl.ds(q0 + 1, size), low - 1 : low + 7, :]
        )
        rows = slice(8 * t, 8 * t + 8)
        stepped = (
            C0[rows][None] * centre
            + A[rows][None] * sides
            + (MERIDIONAL * df_v[...])[None] * poles
        )
        flat = stepped.reshape(size * 8, CH)
        big = flat.astype(BF16)
        small = (flat - big.astype(F32)).astype(BF16)
        wide = jnp.dot(
            jnp.concatenate([big, small], axis=1), R[...], preferred_element_type=F32
        )
        return (flat + (wide[:, :CH] + wide[:, CH:])).reshape(size, 8, CH)

    def smooth(t, i0):
        window = [C[t, i0 + m] for m in range(BLOCK + 2 * MAXB)]
        total = [W[0, t] * window[b + MAXB] for b in range(BLOCK)]
        for k in range(1, MAXB + 1):
            weight = W[k, t]
            for b in range(BLOCK):
                total[b] = total[b] + weight * (window[b + MAXB - k] + window[b + MAXB + k])
        for b in range(BLOCK):
            out[i0 + b, pl.ds(pl.multiple_of(8 * t, 8), 8), :] = total[b]

    def inner(t):
        n = COLS - 2
        steps = (n + CHUNK - 1) // CHUNK

        @pl.loop(0, steps)
        def _(j):
            q0 = HALO + jnp.minimum(j * CHUNK, n - CHUNK)
            C[t, pl.ds(q0, CHUNK)] = couple(t, q0, CHUNK)

        m = COLS - 2 * HALO
        steps = (m + BLOCK - 1) // BLOCK

        @pl.loop(0, steps)
        def _(j):
            smooth(t, HALO + jnp.minimum(j * BLOCK, m - BLOCK))

    def edges(t):
        C[t, 0:HALO] = couple(t, 0, HALO)
        C[t, COLS + MAXB - 1 : COLS + 2 * MAXB] = couple(t, COLS + MAXB - 1, HALO)

        @pl.loop(0, 6)
        def _(j):
            left = jnp.minimum(j * BLOCK, HALO - BLOCK)
            right = COLS - HALO + jnp.minimum((j - 3) * BLOCK, HALO - BLOCK)
            smooth(t, jnp.where(j < 3, left, right))

    def plain(t):
        steps = (COLS + CHUNK - 1) // CHUNK

        @pl.loop(0, steps)
        def _(j):
            i0 = jnp.minimum(j * CHUNK, COLS - CHUNK)
            out[pl.ds(i0, CHUNK), 8 * t : 8 * t + 8, :] = couple(t, i0 + MAXB, CHUNK)

    body.wait()

    @pl.when(polar)
    def _():
        inner(1)
        inner(2)

    pl.when(has_down)(lambda: wait_recv(up))
    pl.when(has_up)(lambda: wait_recv(down))

    @pl.when(polar)
    def _():
        inner(0)
        inner(3)
        pl.when(has_down)(lambda: wait_recv(up_east, up_west))
        pl.when(has_up)(lambda: wait_recv(down_east, down_west))
        wait_recv(*wide[0])
        for t in range(TILES):
            if t + 1 < TILES:
                wait_recv(*wide[t + 1])
            edges(t)

    @pl.when(jnp.logical_not(polar))
    def _():
        wait_recv(*thin)
        for t in range(TILES):
            plain(t)

    pl.when(polar)(lambda: wait_send(*[copy for pair in wide for copy in pair]))
    pl.when(jnp.logical_not(polar))(lambda: wait_send(*thin))
    pl.when(has_up)(lambda: wait_send(up))
    pl.when(has_down)(lambda: wait_send(down))
    pl.when(to_up)(lambda: wait_send(up_east, up_west))
    pl.when(to_down)(lambda: wait_send(down_east, down_west))


def local(
    state, zonal_coef, diffusivity, coupling, filter_rows, band_width, table_index, coef_table
):
    turned = jnp.transpose(state, (1, 0, 2))
    args = (
        turned, zonal_coef[None, :], diffusivity[None, :], coupling,
        filter_rows[None, :], band_width[None, :], table_index[None, :], coef_table,
    )
    updated = pl.pallas_call(
        kernel,
        out_shape=jax.ShapeDtypeStruct((COLS, ROWS, CH), F32),
        in_specs=[pl.BlockSpec(memory_space=pl.ANY)] * len(args),
        out_specs=pl.BlockSpec(memory_space=pltpu.VMEM),
        scratch_shapes=[
            pltpu.VMEM((COLS + 2 * HALO, ROWS + 16, CH), F32),
            pltpu.VMEM((TILES, COLS + 2 * MAXB, 8, CH), F32),
            pltpu.VMEM((MAXB + 1, TILES, 8, CH), F32),
            pltpu.VMEM((ROWS, CH), F32),
            pltpu.VMEM((ROWS, CH), F32),
            pltpu.VMEM((2 * CH, 2 * CH), BF16),
        ]
        + [pltpu.VMEM(a.shape, a.dtype) for a in args[1:]]
        + [
            pltpu.SemaphoreType.DMA((14,)),
            pltpu.SemaphoreType.DMA((14,)),
            pltpu.SemaphoreType.DMA((8,)),
        ],
        compiler_params=pltpu.CompilerParams(
            collective_id=0, has_side_effects=True, vmem_limit_bytes=56 * 1024 * 1024
        ),
    )(*args)
    return jnp.transpose(updated, (1, 0, 2))


def solution(mesh):
    return jax.shard_map(
        local,
        mesh=mesh,
        in_specs=(P("lat", "lon", None), P("lat"), P(), P(), P(), P(), P(), P()),
        out_specs=P("lat", "lon", None),
        check_vma=False,
    )
```

```python
import jax
import jax.numpy as jnp
from jax import lax
from jax.experimental import pallas as pl
from jax.experimental.pallas import tpu as pltpu
from jax.sharding import PartitionSpec as P

MAXB = 16
HALO = MAXB + 1
MERIDIONAL = 0.1
ROWS = 32
COLS = 225
CH = 128
TILES = ROWS // 8
CHUNK = 112
PLAIN = 75
BLOCK = 8
MESH = pl.DeviceIdType.MESH
F32 = jnp.float32
BF16 = jnp.bfloat16


def chunks(total, size):
    return [min(i * size, total - size) for i in range((total + size - 1) // size)]


def kernel(
    st, zc, df, cp, fr, bw, ti, ct, out,
    S, C, W, A, C0, R, zc_v, df_v, cp_v, fr_v, bw_v, ti_v, ct_v, ss, rs, ls,
):
    la = lax.axis_index("lat")
    lo = lax.axis_index("lon")
    east = lax.rem(lo + 1, 16)
    west = lax.rem(lo + 15, 16)

    def is_polar(pos):
        return (pos < 4) | (pos >= 12)

    polar = is_polar(la)
    has_up = la < 15
    has_down = la > 0
    corner_up = has_up & (polar | is_polar(la + 1))
    corner_down = has_down & (polar | is_polar(la - 1))

    barrier = pltpu.get_barrier_semaphore()

    def greet(*who):
        for device in who:
            pl.semaphore_signal(barrier, inc=1, device_id=device, device_id_type=MESH)

    greet((la, east), (la, west))
    pl.when(has_up)(lambda: greet((la + 1, lo)))
    pl.when(has_down)(lambda: greet((la - 1, lo)))
    pl.when(corner_up)(lambda: greet((la + 1, east), (la + 1, west)))
    pl.when(corner_down)(lambda: greet((la - 1, east), (la - 1, west)))

    small = [(zc, zc_v), (df, df_v), (cp, cp_v), (fr, fr_v), (bw, bw_v), (ti, ti_v), (ct, ct_v)]
    loads = [pltpu.make_async_copy(src, dst, ls.at[i]) for i, (src, dst) in enumerate(small)]
    body = pltpu.make_async_copy(st, S.at[HALO : HALO + COLS, 8 : 8 + ROWS], ls.at[7])
    body.start()
    for load in loads:
        load.start()

    def prepare():
        for load in loads:
            load.wait()
        body.wait()

        def iota(shape, dim):
            return lax.broadcasted_iota(jnp.int32, shape, dim)

        def column(values, offset):
            width = values.shape[1]
            pick = iota((ROWS, width), 1) == iota((ROWS, width), 0) + offset
            return jnp.sum(jnp.where(pick, values.astype(F32), 0.0), axis=1, keepdims=True)

        zonal = column(zc_v[...], 0)
        spread = df_v[...]
        A[...] = zonal * spread
        C0[...] = 1.0 - 2.0 * (zonal + MERIDIONAL) * spread
        fine = cp_v[...]
        coarse = fine.astype(BF16)
        rest = (fine - coarse.astype(F32)).astype(BF16)
        both = jnp.concatenate([coarse, rest], axis=1)
        R[...] = jnp.concatenate([both, both], axis=0)

        @pl.when(polar)
        def _():
            first = la * ROWS
            tables = column(ti_v[...], first)
            widths = column(bw_v[...], first)
            same = fr_v[...] == iota((ROWS, fr_v.shape[1]), 0) + first
            listed = jnp.sum(jnp.where(same, 1.0, 0.0), axis=1, keepdims=True) > 0.5
            taps = ct_v.shape[1]
            picked = jnp.zeros((ROWS, taps), F32)
            for table in range(ct_v.shape[0]):
                picked = jnp.where(tables == float(table), ct_v[table : table + 1, :], picked)
            reach = iota((ROWS, taps), 1)
            picked = jnp.where(reach.astype(F32) <= widths, picked, 0.0)
            picked = jnp.where(listed, picked, jnp.where(reach == 0, 1.0, 0.0))
            for k in range(taps):
                W[k] = jnp.broadcast_to(picked[:, k : k + 1], (ROWS, CH)).reshape(TILES, 8, CH)

    def stepped(t, q0, size):
        low = 8 + 8 * t
        centre = S[pl.ds(q0 + 1, size), low : low + 8, :]
        sides = S[pl.ds(q0 + 2, size), low : low + 8, :] + S[pl.ds(q0, size), low : low + 8, :]
        poles = (
            S[pl.ds(q0 + 1, size), low + 1 : low + 9, :]
            + S[pl.ds(q0 + 1, size), low - 1 : low + 7, :]
        )
        rows = slice(8 * t, 8 * t + 8)
        value = (
            C0[rows][None] * centre
            + A[rows][None] * sides
            + (MERIDIONAL * df_v[...])[None] * poles
        )
        return value.reshape(size * 8, CH)

    def couple(*parts):
        flat = [stepped(*part) for part in parts]
        flat = flat[0] if len(flat) == 1 else jnp.concatenate(flat, axis=0)
        big = flat.astype(BF16)
        small = (flat - big.astype(F32)).astype(BF16)
        wide = jnp.dot(
            jnp.concatenate([big, small], axis=1), R[...], preferred_element_type=F32
        )
        flat = flat + (wide[:, :CH] + wide[:, CH:])
        return flat.reshape(flat.shape[0] // 8, 8, CH)

    def smooth(t, i0, size):
        window = [C[t, i0 + m] for m in range(size + 2 * MAXB)]
        total = [W[0, t] * window[b + MAXB] for b in range(size)]
        for k in range(1, MAXB + 1):
            weight = W[k, t]
            for b in range(size):
                total[b] = total[b] + weight * (window[b + MAXB - k] + window[b + MAXB + k])
        for b in range(size):
            out[i0 + b, pl.ds(pl.multiple_of(8 * t, 8), 8), :] = total[b]

    def inner(t):
        n = COLS - 2
        steps = (n + CHUNK - 1) // CHUNK

        @pl.loop(0, steps)
        def _(j):
            q0 = HALO + jnp.minimum(j * CHUNK, n - CHUNK)
            C[t, pl.ds(q0, CHUNK)] = couple((t, q0, CHUNK))

        m = COLS - 2 * HALO
        steps = (m + BLOCK - 1) // BLOCK

        @pl.loop(0, steps)
        def _(j):
            smooth(t, HALO + jnp.minimum(j * BLOCK, m - BLOCK), BLOCK)

    def edges(*tiles):
        far = COLS + MAXB - 1
        parts = [(t, q0, HALO) for t in tiles for q0 in (0, far)]
        value = couple(*parts)
        for i, (t, q0, size) in enumerate(parts):
            C[t, q0 : q0 + size] = value[i * size : i * size + size]
        for t in tiles:

            @pl.loop(0, 2)
            def _(j):
                smooth(t, j * (COLS - HALO), HALO)

    def plain(t):
        @pl.loop(0, COLS // PLAIN)
        def _(j):
            i0 = j * PLAIN
            out[pl.ds(i0, PLAIN), 8 * t : 8 * t + 8, :] = couple((t, i0 + MAXB, PLAIN))

    def ahead():
        prepare()

        @pl.when(polar)
        def _():
            inner(1)
            inner(2)

    early = lax.rem(lo, 8) == 0
    pl.when(early)(ahead)

    count = (
        2
        + jnp.where(has_up, 1, 0)
        + jnp.where(has_down, 1, 0)
        + jnp.where(corner_up, 2, 0)
        + jnp.where(corner_down, 2, 0)
    )
    pl.semaphore_wait(barrier, count)

    def send(src, dst, i, device):
        return pltpu.make_async_remote_copy(
            src_ref=src, dst_ref=dst, send_sem=ss.at[i], recv_sem=rs.at[i],
            device_id=device, device_id_type=MESH,
        )

    last = COLS - HALO
    high = HALO + COLS
    wide = []
    for t in range(TILES):
        here, there = slice(8 * t, 8 * t + 8), slice(8 * t + 8, 8 * t + 16)
        wide.append(
            (
                send(st.at[last:COLS, here], S.at[0:HALO, there], 2 * t, (la, east)),
                send(st.at[0:HALO, here], S.at[high : high + HALO, there], 2 * t + 1, (la, west)),
            )
        )
    thin = (
        send(st.at[COLS - 1 : COLS], S.at[HALO - 1 : HALO, 8 : 8 + ROWS], 0, (la, east)),
        send(st.at[0:1], S.at[high : high + 1, 8 : 8 + ROWS], 1, (la, west)),
    )
    up = send(st.at[:, 31:32], S.at[HALO:high, 7:8], 8, (la + 1, lo))
    down = send(st.at[:, 0:1], S.at[HALO:high, 40:41], 9, (la - 1, lo))
    up_east = send(st.at[last:COLS, 31:32], S.at[0:HALO, 7:8], 10, (la + 1, east))
    up_west = send(st.at[0:HALO, 31:32], S.at[high : high + HALO, 7:8], 11, (la + 1, west))
    down_east = send(st.at[last:COLS, 0:1], S.at[0:HALO, 40:41], 12, (la - 1, east))
    down_west = send(st.at[0:HALO, 0:1], S.at[high : high + HALO, 40:41], 13, (la - 1, west))

    def start(*copies):
        for copy in copies:
            copy.start()

    def wait_send(*copies):
        for copy in copies:
            copy.wait_send()

    def wait_recv(*copies):
        for copy in copies:
            copy.wait_recv()

    pl.when(polar)(lambda: start(*[copy for pair in wide for copy in pair]))
    pl.when(jnp.logical_not(polar))(lambda: start(*thin))
    pl.when(has_up)(lambda: start(up))
    pl.when(has_down)(lambda: start(down))
    to_up = has_up & is_polar(la + 1)
    to_down = has_down & is_polar(la - 1)
    pl.when(to_up)(lambda: start(up_east, up_west))
    pl.when(to_down)(lambda: start(down_east, down_west))

    def clear(row):
        S[:, row : row + 1, :] = jnp.zeros((S.shape[0], 1, CH), F32)

    pl.when(jnp.logical_not(has_down))(lambda: clear(7))
    pl.when(jnp.logical_not(has_up))(lambda: clear(40))

    pl.when(jnp.logical_not(early))(ahead)

    pl.when(has_down)(lambda: wait_recv(up))
    pl.when(has_up)(lambda: wait_recv(down))

    @pl.when(polar)
    def _():
        inner(0)
        inner(3)
        pl.when(has_down)(lambda: wait_recv(up_east, up_west))
        pl.when(has_up)(lambda: wait_recv(down_east, down_west))
        wait_recv(*wide[0])
        wait_recv(*wide[1])
        edges(0)
        wait_recv(*wide[2])
        edges(1)
        wait_recv(*wide[3])
        edges(2, 3)

    @pl.when(jnp.logical_not(polar))
    def _():
        wait_recv(*thin)
        for t in range(TILES):
            plain(t)

    pl.when(polar)(lambda: wait_send(*[copy for pair in wide for copy in pair]))
    pl.when(jnp.logical_not(polar))(lambda: wait_send(*thin))
    pl.when(has_up)(lambda: wait_send(up))
    pl.when(has_down)(lambda: wait_send(down))
    pl.when(to_up)(lambda: wait_send(up_east, up_west))
    pl.when(to_down)(lambda: wait_send(down_east, down_west))


def local(
    state, zonal_coef, diffusivity, coupling, filter_rows, band_width, table_index, coef_table
):
    turned = jnp.transpose(state, (1, 0, 2))
    args = (
        turned, zonal_coef[None, :], diffusivity[None, :], coupling,
        filter_rows[None, :], band_width[None, :], table_index[None, :], coef_table,
    )
    updated = pl.pallas_call(
        kernel,
        out_shape=pltpu.VMEM((COLS, ROWS, CH), F32),
        in_specs=[pl.BlockSpec(memory_space=pl.ANY)] * len(args),
        out_specs=pl.BlockSpec(memory_space=pltpu.VMEM),
        scratch_shapes=[
            pltpu.VMEM((COLS + 2 * HALO, ROWS + 16, CH), F32),
            pltpu.VMEM((TILES, COLS + 2 * MAXB, 8, CH), F32),
            pltpu.VMEM((MAXB + 1, TILES, 8, CH), F32),
            pltpu.VMEM((ROWS, CH), F32),
            pltpu.VMEM((ROWS, CH), F32),
            pltpu.VMEM((2 * CH, 2 * CH), BF16),
        ]
        + [pltpu.VMEM(a.shape, a.dtype) for a in args[1:]]
        + [
            pltpu.SemaphoreType.DMA((14,)),
            pltpu.SemaphoreType.DMA((14,)),
            pltpu.SemaphoreType.DMA((8,)),
        ],
        compiler_params=pltpu.CompilerParams(
            collective_id=0, has_side_effects=True, vmem_limit_bytes=56 * 1024 * 1024
        ),
    )(*args)
    return jnp.transpose(updated, (1, 0, 2))


def solution(mesh):
    return jax.shard_map(
        local,
        mesh=mesh,
        in_specs=(P("lat", "lon", None), P("lat"), P(), P(), P(), P(), P(), P()),
        out_specs=P("lat", "lon", None),
        check_vma=False,
    )
```

```python
import jax
import jax.numpy as jnp
from jax import lax
from jax.experimental import pallas as pl
from jax.experimental.pallas import tpu as pltpu
from jax.sharding import PartitionSpec as P

MAXB = 16
HALO = MAXB + 1
MERIDIONAL = 0.1
ROWS = 32
COLS = 225
CH = 128
TILES = ROWS // 8
CHUNK = 112
PLAIN = 75
BLOCK = 8
MESH = pl.DeviceIdType.MESH
F32 = jnp.float32
BF16 = jnp.bfloat16


def chunks(total, size):
    return [min(i * size, total - size) for i in range((total + size - 1) // size)]


def kernel(
    st, zc, df, cp, fr, bw, ti, ct, out,
    S, C, W, A, C0, R, zc_v, df_v, cp_v, fr_v, bw_v, ti_v, ct_v, ss, rs, ls,
    from_east, from_west,
):
    la = lax.axis_index("lat")
    lo = lax.axis_index("lon")
    east = lax.rem(lo + 1, 16)
    west = lax.rem(lo + 15, 16)

    def is_polar(pos):
        return (pos < 4) | (pos >= 12)

    polar = is_polar(la)
    has_up = la < 15
    has_down = la > 0
    corner_up = has_up & (polar | is_polar(la + 1))
    corner_down = has_down & (polar | is_polar(la - 1))

    barrier = pltpu.get_barrier_semaphore()

    def greet(*who):
        for device in who:
            pl.semaphore_signal(barrier, inc=1, device_id=device, device_id_type=MESH)

    first = lax.rem(lo, 8) == 0
    final = lax.rem(lo, 8) == 7
    middle = jnp.logical_not(first)
    going = jnp.logical_not(final)
    neighbours = 1 + jnp.where(corner_up, 1, 0) + jnp.where(corner_down, 1, 0)

    def tell(semaphore, side):
        def one(device):
            pl.semaphore_signal(semaphore, inc=1, device_id=device, device_id_type=MESH)

        one((la, side))
        pl.when(corner_up)(lambda: one((la + 1, side)))
        pl.when(corner_down)(lambda: one((la - 1, side)))

    pl.when(going)(lambda: tell(barrier, east))
    pl.when(first)(lambda: tell(barrier, west))
    pl.when(has_up)(lambda: greet((la + 1, lo)))
    pl.when(has_down)(lambda: greet((la - 1, lo)))

    small = [(zc, zc_v), (df, df_v), (cp, cp_v), (fr, fr_v), (bw, bw_v), (ti, ti_v), (ct, ct_v)]
    loads = [pltpu.make_async_copy(src, dst, ls.at[i]) for i, (src, dst) in enumerate(small)]
    body = pltpu.make_async_copy(st, S.at[HALO : HALO + COLS, 8 : 8 + ROWS], ls.at[7])
    body.start()
    for load in loads:
        load.start()

    def prepare():
        for load in loads:
            load.wait()
        body.wait()

        def iota(shape, dim):
            return lax.broadcasted_iota(jnp.int32, shape, dim)

        def column(values, offset):
            width = values.shape[1]
            pick = iota((ROWS, width), 1) == iota((ROWS, width), 0) + offset
            return jnp.sum(jnp.where(pick, values.astype(F32), 0.0), axis=1, keepdims=True)

        zonal = column(zc_v[...], 0)
        spread = df_v[...]
        A[...] = zonal * spread
        C0[...] = 1.0 - 2.0 * (zonal + MERIDIONAL) * spread
        fine = cp_v[...]
        coarse = fine.astype(BF16)
        rest = (fine - coarse.astype(F32)).astype(BF16)
        both = jnp.concatenate([coarse, rest], axis=1)
        R[...] = jnp.concatenate([both, both], axis=0)

        @pl.when(polar)
        def _():
            first = la * ROWS
            tables = column(ti_v[...], first)
            widths = column(bw_v[...], first)
            same = fr_v[...] == iota((ROWS, fr_v.shape[1]), 0) + first
            listed = jnp.sum(jnp.where(same, 1.0, 0.0), axis=1, keepdims=True) > 0.5
            taps = ct_v.shape[1]
            picked = jnp.zeros((ROWS, taps), F32)
            for table in range(ct_v.shape[0]):
                picked = jnp.where(tables == float(table), ct_v[table : table + 1, :], picked)
            reach = iota((ROWS, taps), 1)
            picked = jnp.where(reach.astype(F32) <= widths, picked, 0.0)
            picked = jnp.where(listed, picked, jnp.where(reach == 0, 1.0, 0.0))
            for k in range(taps):
                W[k] = jnp.broadcast_to(picked[:, k : k + 1], (ROWS, CH)).reshape(TILES, 8, CH)

    def stepped(t, q0, size):
        low = 8 + 8 * t
        centre = S[pl.ds(q0 + 1, size), low : low + 8, :]
        sides = S[pl.ds(q0 + 2, size), low : low + 8, :] + S[pl.ds(q0, size), low : low + 8, :]
        poles = (
            S[pl.ds(q0 + 1, size), low + 1 : low + 9, :]
            + S[pl.ds(q0 + 1, size), low - 1 : low + 7, :]
        )
        rows = slice(8 * t, 8 * t + 8)
        value = (
            C0[rows][None] * centre
            + A[rows][None] * sides
            + (MERIDIONAL * df_v[...])[None] * poles
        )
        return value.reshape(size * 8, CH)

    def couple(*parts):
        flat = [stepped(*part) for part in parts]
        flat = flat[0] if len(flat) == 1 else jnp.concatenate(flat, axis=0)
        big = flat.astype(BF16)
        small = (flat - big.astype(F32)).astype(BF16)
        wide = jnp.dot(
            jnp.concatenate([big, small], axis=1), R[...], preferred_element_type=F32
        )
        flat = flat + (wide[:, :CH] + wide[:, CH:])
        return flat.reshape(flat.shape[0] // 8, 8, CH)

    def smooth(t, i0, size):
        window = [C[t, i0 + m] for m in range(size + 2 * MAXB)]
        total = [W[0, t] * window[b + MAXB] for b in range(size)]
        for k in range(1, MAXB + 1):
            weight = W[k, t]
            for b in range(size):
                total[b] = total[b] + weight * (window[b + MAXB - k] + window[b + MAXB + k])
        for b in range(size):
            out[i0 + b, pl.ds(pl.multiple_of(8 * t, 8), 8), :] = total[b]

    def inner(t):
        n = COLS - 2
        steps = (n + CHUNK - 1) // CHUNK

        @pl.loop(0, steps)
        def _(j):
            q0 = HALO + jnp.minimum(j * CHUNK, n - CHUNK)
            C[t, pl.ds(q0, CHUNK)] = couple((t, q0, CHUNK))

        m = COLS - 2 * HALO
        steps = (m + BLOCK - 1) // BLOCK

        @pl.loop(0, steps)
        def _(j):
            smooth(t, HALO + jnp.minimum(j * BLOCK, m - BLOCK), BLOCK)

    def edges(*tiles):
        far = COLS + MAXB - 1
        parts = [(t, q0, HALO) for t in tiles for q0 in (0, far)]
        value = couple(*parts)
        for i, (t, q0, size) in enumerate(parts):
            C[t, q0 : q0 + size] = value[i * size : i * size + size]
        for t in tiles:

            @pl.loop(0, 2)
            def _(j):
                smooth(t, j * (COLS - HALO), HALO)

    def plain(t):
        @pl.loop(0, COLS // PLAIN)
        def _(j):
            i0 = j * PLAIN
            out[pl.ds(i0, PLAIN), 8 * t : 8 * t + 8, :] = couple((t, i0 + MAXB, PLAIN))

    def ahead():
        prepare()

        @pl.when(polar)
        def _():
            inner(1)
            inner(2)

    count = (
        jnp.where(has_up, 1, 0)
        + jnp.where(has_down, 1, 0)
        + jnp.where(first, 0, neighbours)
        + jnp.where(final, neighbours, 0)
    )
    pl.semaphore_wait(barrier, count)

    def send(src, dst, i, device):
        return pltpu.make_async_remote_copy(
            src_ref=src, dst_ref=dst, send_sem=ss.at[i], recv_sem=rs.at[i],
            device_id=device, device_id_type=MESH,
        )

    last = COLS - HALO
    high = HALO + COLS
    wide = []
    for t in range(TILES):
        here, there = slice(8 * t, 8 * t + 8), slice(8 * t + 8, 8 * t + 16)
        wide.append(
            (
                send(st.at[last:COLS, here], S.at[0:HALO, there], 2 * t, (la, east)),
                send(st.at[0:HALO, here], S.at[high : high + HALO, there], 2 * t + 1, (la, west)),
            )
        )
    thin = (
        send(st.at[COLS - 1 : COLS], S.at[HALO - 1 : HALO, 8 : 8 + ROWS], 0, (la, east)),
        send(st.at[0:1], S.at[high : high + 1, 8 : 8 + ROWS], 1, (la, west)),
    )
    up = send(st.at[:, 31:32], S.at[HALO:high, 7:8], 8, (la + 1, lo))
    down = send(st.at[:, 0:1], S.at[HALO:high, 40:41], 9, (la - 1, lo))
    up_east = send(st.at[last:COLS, 31:32], S.at[0:HALO, 7:8], 10, (la + 1, east))
    up_west = send(st.at[0:HALO, 31:32], S.at[high : high + HALO, 7:8], 11, (la + 1, west))
    down_east = send(st.at[last:COLS, 0:1], S.at[0:HALO, 40:41], 12, (la - 1, east))
    down_west = send(st.at[0:HALO, 0:1], S.at[high : high + HALO, 40:41], 13, (la - 1, west))

    def start(*copies):
        for copy in copies:
            copy.start()

    def wait_send(*copies):
        for copy in copies:
            copy.wait_send()

    def wait_recv(*copies):
        for copy in copies:
            copy.wait_recv()

    to_up = has_up & is_polar(la + 1)
    to_down = has_down & is_polar(la - 1)

    def start_east():
        pl.when(polar)(lambda: start(*[pair[0] for pair in wide]))
        pl.when(jnp.logical_not(polar))(lambda: start(thin[0]))
        pl.when(to_up)(lambda: start(up_east))
        pl.when(to_down)(lambda: start(down_east))

    def start_west():
        pl.when(polar)(lambda: start(*[pair[1] for pair in wide]))
        pl.when(jnp.logical_not(polar))(lambda: start(thin[1]))
        pl.when(to_up)(lambda: start(up_west))
        pl.when(to_down)(lambda: start(down_west))

    @pl.when(final)
    def _():
        start_east()
        tell(from_west, east)

    @pl.when(middle)
    def _():
        tell(from_east, west)
        start_west()

    pl.when(has_up)(lambda: start(up))
    pl.when(has_down)(lambda: start(down))

    @pl.when(going)
    def _():
        pl.semaphore_wait(from_east, neighbours)
        start_east()

    def clear(row):
        S[:, row : row + 1, :] = jnp.zeros((S.shape[0], 1, CH), F32)

    pl.when(jnp.logical_not(has_down))(lambda: clear(7))
    pl.when(jnp.logical_not(has_up))(lambda: clear(40))

    ahead()

    @pl.when(first)
    def _():
        pl.semaphore_wait(from_west, neighbours)
        start_west()

    pl.when(has_down)(lambda: wait_recv(up))
    pl.when(has_up)(lambda: wait_recv(down))

    @pl.when(polar)
    def _():
        inner(0)
        inner(3)
        pl.when(has_down)(lambda: wait_recv(up_east, up_west))
        pl.when(has_up)(lambda: wait_recv(down_east, down_west))
        wait_recv(*wide[0])
        wait_recv(*wide[1])
        edges(0)
        wait_recv(*wide[2])
        edges(1)
        wait_recv(*wide[3])
        edges(2, 3)

    @pl.when(jnp.logical_not(polar))
    def _():
        wait_recv(*thin)
        for t in range(TILES):
            plain(t)

    pl.when(polar)(lambda: wait_send(*[copy for pair in wide for copy in pair]))
    pl.when(jnp.logical_not(polar))(lambda: wait_send(*thin))
    pl.when(has_up)(lambda: wait_send(up))
    pl.when(has_down)(lambda: wait_send(down))
    pl.when(to_up)(lambda: wait_send(up_east, up_west))
    pl.when(to_down)(lambda: wait_send(down_east, down_west))


def local(
    state, zonal_coef, diffusivity, coupling, filter_rows, band_width, table_index, coef_table
):
    turned = jnp.transpose(state, (1, 0, 2))
    args = (
        turned, zonal_coef[None, :], diffusivity[None, :], coupling,
        filter_rows[None, :], band_width[None, :], table_index[None, :], coef_table,
    )
    updated = pl.pallas_call(
        kernel,
        out_shape=pltpu.VMEM((COLS, ROWS, CH), F32),
        in_specs=[pl.BlockSpec(memory_space=pl.ANY)] * len(args),
        out_specs=pl.BlockSpec(memory_space=pltpu.VMEM),
        scratch_shapes=[
            pltpu.VMEM((COLS + 2 * HALO, ROWS + 16, CH), F32),
            pltpu.VMEM((TILES, COLS + 2 * MAXB, 8, CH), F32),
            pltpu.VMEM((MAXB + 1, TILES, 8, CH), F32),
            pltpu.VMEM((ROWS, CH), F32),
            pltpu.VMEM((ROWS, CH), F32),
            pltpu.VMEM((2 * CH, 2 * CH), BF16),
        ]
        + [pltpu.VMEM(a.shape, a.dtype) for a in args[1:]]
        + [
            pltpu.SemaphoreType.DMA((14,)),
            pltpu.SemaphoreType.DMA((14,)),
            pltpu.SemaphoreType.DMA((8,)),
            pltpu.SemaphoreType.REGULAR,
            pltpu.SemaphoreType.REGULAR,
        ],
        compiler_params=pltpu.CompilerParams(
            collective_id=0, has_side_effects=True, vmem_limit_bytes=56 * 1024 * 1024
        ),
    )(*args)
    return jnp.transpose(updated, (1, 0, 2))


def solution(mesh):
    return jax.shard_map(
        local,
        mesh=mesh,
        in_specs=(P("lat", "lon", None), P("lat"), P(), P(), P(), P(), P(), P()),
        out_specs=P("lat", "lon", None),
        check_vma=False,
    )
```

```python
import jax
import jax.numpy as jnp
from jax import lax
from jax.experimental import pallas as pl
from jax.experimental.pallas import tpu as pltpu
from jax.sharding import PartitionSpec as P

MAXB = 16
HALO = MAXB + 1
MERIDIONAL = 0.1
ROWS = 32
COLS = 225
CH = 128
TILES = ROWS // 8
CHUNK = 112
PLAIN = 75
BLOCK = 8
MESH = pl.DeviceIdType.MESH
F32 = jnp.float32
BF16 = jnp.bfloat16


def chunks(total, size):
    return [min(i * size, total - size) for i in range((total + size - 1) // size)]


def kernel(
    st, zc, df, cp, fr, bw, ti, ct, out,
    S, C, W, A, C0, R, zc_v, df_v, cp_v, fr_v, bw_v, ti_v, ct_v, ss, rs, ls,
    from_east, from_west,
):
    la = lax.axis_index("lat")
    lo = lax.axis_index("lon")
    east = lax.rem(lo + 1, 16)
    west = lax.rem(lo + 15, 16)

    def is_polar(pos):
        return (pos < 4) | (pos >= 12)

    polar = is_polar(la)
    has_up = la < 15
    has_down = la > 0
    corner_up = has_up & (polar | is_polar(la + 1))
    corner_down = has_down & (polar | is_polar(la - 1))

    barrier = pltpu.get_barrier_semaphore()

    def greet(*who):
        for device in who:
            pl.semaphore_signal(barrier, inc=1, device_id=device, device_id_type=MESH)

    first = lax.rem(lo, 8) == 0
    final = lax.rem(lo, 8) == 7
    middle = jnp.logical_not(first)
    going = jnp.logical_not(final)
    neighbours = 1 + jnp.where(corner_up, 1, 0) + jnp.where(corner_down, 1, 0)

    def tell(semaphore, side):
        def one(device):
            pl.semaphore_signal(semaphore, inc=1, device_id=device, device_id_type=MESH)

        one((la, side))
        pl.when(corner_up)(lambda: one((la + 1, side)))
        pl.when(corner_down)(lambda: one((la - 1, side)))

    pl.when(going)(lambda: tell(barrier, east))
    pl.when(first)(lambda: tell(barrier, west))
    pl.when(has_up)(lambda: greet((la + 1, lo)))
    pl.when(has_down)(lambda: greet((la - 1, lo)))

    small = [(zc, zc_v), (df, df_v), (cp, cp_v), (fr, fr_v), (bw, bw_v), (ti, ti_v), (ct, ct_v)]
    loads = [pltpu.make_async_copy(src, dst, ls.at[i]) for i, (src, dst) in enumerate(small)]
    body = pltpu.make_async_copy(st, S.at[HALO : HALO + COLS, 8 : 8 + ROWS], ls.at[7])

    def fetch():
        body.start()
        for load in loads:
            load.start()

    pl.when(first)(fetch)

    def prepare():
        for load in loads:
            load.wait()
        body.wait()

        def iota(shape, dim):
            return lax.broadcasted_iota(jnp.int32, shape, dim)

        def column(values, offset):
            width = values.shape[1]
            pick = iota((ROWS, width), 1) == iota((ROWS, width), 0) + offset
            return jnp.sum(jnp.where(pick, values.astype(F32), 0.0), axis=1, keepdims=True)

        zonal = column(zc_v[...], 0)
        spread = df_v[...]
        A[...] = zonal * spread
        C0[...] = 1.0 - 2.0 * (zonal + MERIDIONAL) * spread
        fine = cp_v[...]
        coarse = fine.astype(BF16)
        rest = (fine - coarse.astype(F32)).astype(BF16)
        both = jnp.concatenate([coarse, rest], axis=1)
        R[...] = jnp.concatenate([both, both], axis=0)

        @pl.when(polar)
        def _():
            first = la * ROWS
            tables = column(ti_v[...], first)
            widths = column(bw_v[...], first)
            same = fr_v[...] == iota((ROWS, fr_v.shape[1]), 0) + first
            listed = jnp.sum(jnp.where(same, 1.0, 0.0), axis=1, keepdims=True) > 0.5
            taps = ct_v.shape[1]
            picked = jnp.zeros((ROWS, taps), F32)
            for table in range(ct_v.shape[0]):
                picked = jnp.where(tables == float(table), ct_v[table : table + 1, :], picked)
            reach = iota((ROWS, taps), 1)
            picked = jnp.where(reach.astype(F32) <= widths, picked, 0.0)
            picked = jnp.where(listed, picked, jnp.where(reach == 0, 1.0, 0.0))
            for k in range(taps):
                W[k] = jnp.broadcast_to(picked[:, k : k + 1], (ROWS, CH)).reshape(TILES, 8, CH)

    def stepped(t, q0, size):
        low = 8 + 8 * t
        centre = S[pl.ds(q0 + 1, size), low : low + 8, :]
        sides = S[pl.ds(q0 + 2, size), low : low + 8, :] + S[pl.ds(q0, size), low : low + 8, :]
        poles = (
            S[pl.ds(q0 + 1, size), low + 1 : low + 9, :]
            + S[pl.ds(q0 + 1, size), low - 1 : low + 7, :]
        )
        rows = slice(8 * t, 8 * t + 8)
        value = (
            C0[rows][None] * centre
            + A[rows][None] * sides
            + (MERIDIONAL * df_v[...])[None] * poles
        )
        return value.reshape(size * 8, CH)

    def couple(*parts):
        flat = [stepped(*part) for part in parts]
        flat = flat[0] if len(flat) == 1 else jnp.concatenate(flat, axis=0)
        big = flat.astype(BF16)
        small = (flat - big.astype(F32)).astype(BF16)
        wide = jnp.dot(
            jnp.concatenate([big, small], axis=1), R[...], preferred_element_type=F32
        )
        flat = flat + (wide[:, :CH] + wide[:, CH:])
        return flat.reshape(flat.shape[0] // 8, 8, CH)

    def smooth(t, i0, size):
        window = [C[t, i0 + m] for m in range(size + 2 * MAXB)]
        total = [W[0, t] * window[b + MAXB] for b in range(size)]
        for k in range(1, MAXB + 1):
            weight = W[k, t]
            for b in range(size):
                total[b] = total[b] + weight * (window[b + MAXB - k] + window[b + MAXB + k])
        for b in range(size):
            out[i0 + b, pl.ds(pl.multiple_of(8 * t, 8), 8), :] = total[b]

    def inner(t):
        n = COLS - 2
        steps = (n + CHUNK - 1) // CHUNK

        @pl.loop(0, steps)
        def _(j):
            q0 = HALO + jnp.minimum(j * CHUNK, n - CHUNK)
            C[t, pl.ds(q0, CHUNK)] = couple((t, q0, CHUNK))

        m = COLS - 2 * HALO
        steps = (m + BLOCK - 1) // BLOCK

        @pl.loop(0, steps)
        def _(j):
            smooth(t, HALO + jnp.minimum(j * BLOCK, m - BLOCK), BLOCK)

    def edges(*tiles):
        far = COLS + MAXB - 1
        parts = [(t, q0, HALO) for t in tiles for q0 in (0, far)]
        value = couple(*parts)
        for i, (t, q0, size) in enumerate(parts):
            C[t, q0 : q0 + size] = value[i * size : i * size + size]
        for t in tiles:

            @pl.loop(0, 2)
            def _(j):
                smooth(t, j * (COLS - HALO), HALO)

    def plain(t):
        @pl.loop(0, COLS // PLAIN)
        def _(j):
            i0 = j * PLAIN
            out[pl.ds(i0, PLAIN), 8 * t : 8 * t + 8, :] = couple((t, i0 + MAXB, PLAIN))

    def ahead():
        prepare()

        @pl.when(polar)
        def _():
            inner(1)
            inner(2)

    count = (
        jnp.where(has_up, 1, 0)
        + jnp.where(has_down, 1, 0)
        + jnp.where(first, 0, neighbours)
        + jnp.where(final, neighbours, 0)
    )
    pl.semaphore_wait(barrier, count)

    def send(src, dst, i, device):
        return pltpu.make_async_remote_copy(
            src_ref=src, dst_ref=dst, send_sem=ss.at[i], recv_sem=rs.at[i],
            device_id=device, device_id_type=MESH,
        )

    last = COLS - HALO
    high = HALO + COLS
    wide = []
    for t in range(TILES):
        here, there = slice(8 * t, 8 * t + 8), slice(8 * t + 8, 8 * t + 16)
        wide.append(
            (
                send(st.at[last:COLS, here], S.at[0:HALO, there], 2 * t, (la, east)),
                send(st.at[0:HALO, here], S.at[high : high + HALO, there], 2 * t + 1, (la, west)),
            )
        )
    thin = (
        send(st.at[COLS - 1 : COLS], S.at[HALO - 1 : HALO, 8 : 8 + ROWS], 0, (la, east)),
        send(st.at[0:1], S.at[high : high + 1, 8 : 8 + ROWS], 1, (la, west)),
    )
    up = send(st.at[:, 31:32], S.at[HALO:high, 7:8], 8, (la + 1, lo))
    down = send(st.at[:, 0:1], S.at[HALO:high, 40:41], 9, (la - 1, lo))
    up_east = send(st.at[last:COLS, 31:32], S.at[0:HALO, 7:8], 10, (la + 1, east))
    up_west = send(st.at[0:HALO, 31:32], S.at[high : high + HALO, 7:8], 11, (la + 1, west))
    down_east = send(st.at[last:COLS, 0:1], S.at[0:HALO, 40:41], 12, (la - 1, east))
    down_west = send(st.at[0:HALO, 0:1], S.at[high : high + HALO, 40:41], 13, (la - 1, west))

    def start(*copies):
        for copy in copies:
            copy.start()

    def wait_send(*copies):
        for copy in copies:
            copy.wait_send()

    def wait_recv(*copies):
        for copy in copies:
            copy.wait_recv()

    to_up = has_up & is_polar(la + 1)
    to_down = has_down & is_polar(la - 1)

    def start_east():
        pl.when(polar)(lambda: start(*[pair[0] for pair in wide]))
        pl.when(jnp.logical_not(polar))(lambda: start(thin[0]))
        pl.when(to_up)(lambda: start(up_east))
        pl.when(to_down)(lambda: start(down_east))

    def start_west():
        pl.when(polar)(lambda: start(*[pair[1] for pair in wide]))
        pl.when(jnp.logical_not(polar))(lambda: start(thin[1]))
        pl.when(to_up)(lambda: start(up_west))
        pl.when(to_down)(lambda: start(down_west))

    @pl.when(final)
    def _():
        start_east()
        tell(from_west, east)

    @pl.when(middle)
    def _():
        tell(from_east, west)
        start_west()

    pl.when(has_up)(lambda: start(up))
    pl.when(has_down)(lambda: start(down))
    pl.when(middle)(fetch)

    @pl.when(going)
    def _():
        pl.semaphore_wait(from_east, neighbours)
        start_east()

    def clear(row):
        S[:, row : row + 1, :] = jnp.zeros((S.shape[0], 1, CH), F32)

    pl.when(jnp.logical_not(has_down))(lambda: clear(7))
    pl.when(jnp.logical_not(has_up))(lambda: clear(40))

    ahead()

    @pl.when(first)
    def _():
        pl.semaphore_wait(from_west, neighbours)
        start_west()

    pl.when(has_down)(lambda: wait_recv(up))
    pl.when(has_up)(lambda: wait_recv(down))

    @pl.when(polar)
    def _():
        inner(0)
        inner(3)
        pl.when(has_down)(lambda: wait_recv(up_east, up_west))
        pl.when(has_up)(lambda: wait_recv(down_east, down_west))
        wait_recv(*wide[0])
        wait_recv(*wide[1])
        edges(0)
        wait_recv(*wide[2])
        edges(1)
        wait_recv(*wide[3])
        edges(2, 3)

    @pl.when(jnp.logical_not(polar))
    def _():
        wait_recv(*thin)
        for t in range(TILES):
            plain(t)

    pl.when(polar)(lambda: wait_send(*[copy for pair in wide for copy in pair]))
    pl.when(jnp.logical_not(polar))(lambda: wait_send(*thin))
    pl.when(has_up)(lambda: wait_send(up))
    pl.when(has_down)(lambda: wait_send(down))
    pl.when(to_up)(lambda: wait_send(up_east, up_west))
    pl.when(to_down)(lambda: wait_send(down_east, down_west))


def local(
    state, zonal_coef, diffusivity, coupling, filter_rows, band_width, table_index, coef_table
):
    turned = jnp.transpose(state, (1, 0, 2))
    args = (
        turned, zonal_coef[None, :], diffusivity[None, :], coupling,
        filter_rows[None, :], band_width[None, :], table_index[None, :], coef_table,
    )
    updated = pl.pallas_call(
        kernel,
        out_shape=pltpu.VMEM((COLS, ROWS, CH), F32),
        in_specs=[pl.BlockSpec(memory_space=pl.ANY)] * len(args),
        out_specs=pl.BlockSpec(memory_space=pltpu.VMEM),
        scratch_shapes=[
            pltpu.VMEM((COLS + 2 * HALO, ROWS + 16, CH), F32),
            pltpu.VMEM((TILES, COLS + 2 * MAXB, 8, CH), F32),
            pltpu.VMEM((MAXB + 1, TILES, 8, CH), F32),
            pltpu.VMEM((ROWS, CH), F32),
            pltpu.VMEM((ROWS, CH), F32),
            pltpu.VMEM((2 * CH, 2 * CH), BF16),
        ]
        + [pltpu.VMEM(a.shape, a.dtype) for a in args[1:]]
        + [
            pltpu.SemaphoreType.DMA((14,)),
            pltpu.SemaphoreType.DMA((14,)),
            pltpu.SemaphoreType.DMA((8,)),
            pltpu.SemaphoreType.REGULAR,
            pltpu.SemaphoreType.REGULAR,
        ],
        compiler_params=pltpu.CompilerParams(
            collective_id=0, has_side_effects=True, vmem_limit_bytes=56 * 1024 * 1024
        ),
    )(*args)
    return jnp.transpose(updated, (1, 0, 2))


def solution(mesh):
    return jax.shard_map(
        local,
        mesh=mesh,
        in_specs=(P("lat", "lon", None), P("lat"), P(), P(), P(), P(), P(), P()),
        out_specs=P("lat", "lon", None),
        check_vma=False,
    )
```

```python
import jax
import jax.numpy as jnp
from jax import lax
from jax.experimental import pallas as pl
from jax.experimental.pallas import tpu as pltpu
from jax.sharding import PartitionSpec as P

MAXB = 16
HALO = MAXB + 1
MERIDIONAL = 0.1
ROWS = 32
COLS = 225
CH = 128
TILES = ROWS // 8
CHUNK = 112
PLAIN = 75
BLOCK = 8
MESH = pl.DeviceIdType.MESH
F32 = jnp.float32
BF16 = jnp.bfloat16


def chunks(total, size):
    return [min(i * size, total - size) for i in range((total + size - 1) // size)]


def kernel(
    st, zc, df, cp, fr, bw, ti, ct, out,
    S, C, W, A, C0, R, zc_v, df_v, cp_v, fr_v, bw_v, ti_v, ct_v, ss, rs, ls,
    from_east, from_west, from_lat,
):
    la = lax.axis_index("lat")
    lo = lax.axis_index("lon")
    east = lax.rem(lo + 1, 16)
    west = lax.rem(lo + 15, 16)

    def is_polar(pos):
        return (pos < 4) | (pos >= 12)

    polar = is_polar(la)
    has_up = la < 15
    has_down = la > 0
    corner_up = has_up & (polar | is_polar(la + 1))
    corner_down = has_down & (polar | is_polar(la - 1))

    barrier = pltpu.get_barrier_semaphore()

    first = lax.rem(lo, 8) == 0
    final = lax.rem(lo, 8) == 7
    middle = jnp.logical_not(first)
    going = jnp.logical_not(final)
    neighbours = 1 + jnp.where(corner_up, 1, 0) + jnp.where(corner_down, 1, 0)

    def tell(semaphore, side):
        def one(device):
            pl.semaphore_signal(semaphore, inc=1, device_id=device, device_id_type=MESH)

        one((la, side))
        pl.when(corner_up)(lambda: one((la + 1, side)))
        pl.when(corner_down)(lambda: one((la - 1, side)))

    pl.when(going)(lambda: tell(barrier, east))
    pl.when(first)(lambda: tell(barrier, west))
    odd = lax.rem(la, 2) == 1
    even = jnp.logical_not(odd)
    beside = jnp.where(has_up, 1, 0) + jnp.where(has_down, 1, 0)

    def tell_lat(semaphore):
        def one(device):
            pl.semaphore_signal(semaphore, inc=1, device_id=device, device_id_type=MESH)

        pl.when(has_up)(lambda: one((la + 1, lo)))
        pl.when(has_down)(lambda: one((la - 1, lo)))

    pl.when(odd)(lambda: tell_lat(barrier))

    small = [(zc, zc_v), (df, df_v), (cp, cp_v), (fr, fr_v), (bw, bw_v), (ti, ti_v), (ct, ct_v)]
    loads = [pltpu.make_async_copy(src, dst, ls.at[i]) for i, (src, dst) in enumerate(small)]
    body = pltpu.make_async_copy(st, S.at[HALO : HALO + COLS, 8 : 8 + ROWS], ls.at[7])

    def fetch():
        body.start()
        for load in loads:
            load.start()

    pl.when(first)(fetch)

    def prepare():
        for load in loads:
            load.wait()
        body.wait()

        def iota(shape, dim):
            return lax.broadcasted_iota(jnp.int32, shape, dim)

        def column(values, offset):
            width = values.shape[1]
            pick = iota((ROWS, width), 1) == iota((ROWS, width), 0) + offset
            return jnp.sum(jnp.where(pick, values.astype(F32), 0.0), axis=1, keepdims=True)

        zonal = column(zc_v[...], 0)
        spread = df_v[...]
        A[...] = zonal * spread
        C0[...] = 1.0 - 2.0 * (zonal + MERIDIONAL) * spread
        fine = cp_v[...]
        coarse = fine.astype(BF16)
        rest = (fine - coarse.astype(F32)).astype(BF16)
        both = jnp.concatenate([coarse, rest], axis=1)
        R[...] = jnp.concatenate([both, both], axis=0)

        @pl.when(polar)
        def _():
            first = la * ROWS
            tables = column(ti_v[...], first)
            widths = column(bw_v[...], first)
            same = fr_v[...] == iota((ROWS, fr_v.shape[1]), 0) + first
            listed = jnp.sum(jnp.where(same, 1.0, 0.0), axis=1, keepdims=True) > 0.5
            taps = ct_v.shape[1]
            picked = jnp.zeros((ROWS, taps), F32)
            for table in range(ct_v.shape[0]):
                picked = jnp.where(tables == float(table), ct_v[table : table + 1, :], picked)
            reach = iota((ROWS, taps), 1)
            picked = jnp.where(reach.astype(F32) <= widths, picked, 0.0)
            picked = jnp.where(listed, picked, jnp.where(reach == 0, 1.0, 0.0))
            for k in range(taps):
                W[k] = jnp.broadcast_to(picked[:, k : k + 1], (ROWS, CH)).reshape(TILES, 8, CH)

    def stepped(t, q0, size):
        low = 8 + 8 * t
        centre = S[pl.ds(q0 + 1, size), low : low + 8, :]
        sides = S[pl.ds(q0 + 2, size), low : low + 8, :] + S[pl.ds(q0, size), low : low + 8, :]
        poles = (
            S[pl.ds(q0 + 1, size), low + 1 : low + 9, :]
            + S[pl.ds(q0 + 1, size), low - 1 : low + 7, :]
        )
        rows = slice(8 * t, 8 * t + 8)
        value = (
            C0[rows][None] * centre
            + A[rows][None] * sides
            + (MERIDIONAL * df_v[...])[None] * poles
        )
        return value.reshape(size * 8, CH)

    def couple(*parts):
        flat = [stepped(*part) for part in parts]
        flat = flat[0] if len(flat) == 1 else jnp.concatenate(flat, axis=0)
        big = flat.astype(BF16)
        small = (flat - big.astype(F32)).astype(BF16)
        wide = jnp.dot(
            jnp.concatenate([big, small], axis=1), R[...], preferred_element_type=F32
        )
        flat = flat + (wide[:, :CH] + wide[:, CH:])
        return flat.reshape(flat.shape[0] // 8, 8, CH)

    def smooth(t, i0, size):
        window = [C[t, i0 + m] for m in range(size + 2 * MAXB)]
        total = [W[0, t] * window[b + MAXB] for b in range(size)]
        for k in range(1, MAXB + 1):
            weight = W[k, t]
            for b in range(size):
                total[b] = total[b] + weight * (window[b + MAXB - k] + window[b + MAXB + k])
        for b in range(size):
            out[i0 + b, pl.ds(pl.multiple_of(8 * t, 8), 8), :] = total[b]

    def inner(t):
        n = COLS - 2
        steps = (n + CHUNK - 1) // CHUNK

        @pl.loop(0, steps)
        def _(j):
            q0 = HALO + jnp.minimum(j * CHUNK, n - CHUNK)
            C[t, pl.ds(q0, CHUNK)] = couple((t, q0, CHUNK))

        m = COLS - 2 * HALO
        steps = (m + BLOCK - 1) // BLOCK

        @pl.loop(0, steps)
        def _(j):
            smooth(t, HALO + jnp.minimum(j * BLOCK, m - BLOCK), BLOCK)

    def edge(t, right, known):
        place = [COLS - 1 - i if right else i for i in range(HALO)]
        rows = pl.ds(pl.multiple_of(8 * t, 8), 8)
        most = HALO + 2 * MAXB
        wanted = range(HALO, most) if known else range(HALO)
        source = {q: C[t, COLS + 2 * MAXB - 1 - q if right else q] for q in wanted}
        total = [None if known else out[i, rows, :] for i in place]
        for k in range(MAXB + 1):
            weight = W[k, t]
            for i in range(HALO):
                reached = sorted({i + MAXB - k, i + MAXB + k})
                values = [source[q] for q in reached if q in source]
                if values:
                    value = weight * (values[0] if len(values) == 1 else values[0] + values[1])
                    total[i] = value if total[i] is None else total[i] + value
        for i in range(HALO):
            out[place[i], rows, :] = total[i]

    def both_edges(known):
        @pl.loop(0, TILES)
        def _(t):
            edge(t, False, known)
            edge(t, True, known)

    def close():
        far = COLS + MAXB - 1
        parts = [(t, q0, HALO) for t in range(TILES) for q0 in (0, far)]
        value = couple(*parts)
        for i, (t, q0, size) in enumerate(parts):
            C[t, q0 : q0 + size] = value[i * size : i * size + size]
        both_edges(False)

    def plain(t):
        @pl.loop(0, COLS // PLAIN)
        def _(j):
            i0 = j * PLAIN
            out[pl.ds(i0, PLAIN), 8 * t : 8 * t + 8, :] = couple((t, i0 + MAXB, PLAIN))

    def ahead():
        prepare()

        @pl.when(polar)
        def _():
            inner(1)
            inner(2)

    count = (
        jnp.where(odd, 0, beside)
        + jnp.where(first, 0, neighbours)
        + jnp.where(final, neighbours, 0)
    )
    pl.when(count > 0)(lambda: pl.semaphore_wait(barrier, count))

    def send(src, dst, i, device):
        return pltpu.make_async_remote_copy(
            src_ref=src, dst_ref=dst, send_sem=ss.at[i], recv_sem=rs.at[i],
            device_id=device, device_id_type=MESH,
        )

    last = COLS - HALO
    high = HALO + COLS
    wide = (
        send(st.at[last:COLS], S.at[0:HALO, 8 : 8 + ROWS], 2, (la, east)),
        send(st.at[0:HALO], S.at[high : high + HALO, 8 : 8 + ROWS], 3, (la, west)),
    )
    thin = (
        send(st.at[COLS - 1 : COLS], S.at[HALO - 1 : HALO, 8 : 8 + ROWS], 0, (la, east)),
        send(st.at[0:1], S.at[high : high + 1, 8 : 8 + ROWS], 1, (la, west)),
    )
    up = send(st.at[:, 31:32], S.at[HALO:high, 7:8], 8, (la + 1, lo))
    down = send(st.at[:, 0:1], S.at[HALO:high, 40:41], 9, (la - 1, lo))
    up_east = send(st.at[last:COLS, 31:32], S.at[0:HALO, 7:8], 10, (la + 1, east))
    up_west = send(st.at[0:HALO, 31:32], S.at[high : high + HALO, 7:8], 11, (la + 1, west))
    down_east = send(st.at[last:COLS, 0:1], S.at[0:HALO, 40:41], 12, (la - 1, east))
    down_west = send(st.at[0:HALO, 0:1], S.at[high : high + HALO, 40:41], 13, (la - 1, west))

    def start(*copies):
        for copy in copies:
            copy.start()

    def wait_send(*copies):
        for copy in copies:
            copy.wait_send()

    def wait_recv(*copies):
        for copy in copies:
            copy.wait_recv()

    to_up = has_up & is_polar(la + 1)
    to_down = has_down & is_polar(la - 1)

    def start_east():
        pl.when(polar)(lambda: start(wide[0]))
        pl.when(jnp.logical_not(polar))(lambda: start(thin[0]))
        pl.when(to_up)(lambda: start(up_east))
        pl.when(to_down)(lambda: start(down_east))

    def start_west():
        pl.when(polar)(lambda: start(wide[1]))
        pl.when(jnp.logical_not(polar))(lambda: start(thin[1]))
        pl.when(to_up)(lambda: start(up_west))
        pl.when(to_down)(lambda: start(down_west))

    def start_lat():
        pl.when(has_up)(lambda: start(up))
        pl.when(has_down)(lambda: start(down))

    @pl.when(final)
    def _():
        start_east()
        tell(from_west, east)

    @pl.when(middle)
    def _():
        tell(from_east, west)
        start_west()

    pl.when(middle)(fetch)

    @pl.when(even)
    def _():
        tell_lat(from_lat)
        start_lat()

    @pl.when(going)
    def _():
        pl.semaphore_wait(from_east, neighbours)
        start_east()

    @pl.when(odd)
    def _():
        pl.semaphore_wait(from_lat, beside)
        start_lat()

    def clear(row):
        S[:, row : row + 1, :] = jnp.zeros((S.shape[0], 1, CH), F32)

    pl.when(jnp.logical_not(has_down))(lambda: clear(7))
    pl.when(jnp.logical_not(has_up))(lambda: clear(40))

    ahead()

    @pl.when(first)
    def _():
        pl.semaphore_wait(from_west, neighbours)
        start_west()

    pl.when(has_down)(lambda: wait_recv(up))
    pl.when(has_up)(lambda: wait_recv(down))

    @pl.when(polar)
    def _():
        inner(0)
        inner(3)
        both_edges(True)
        pl.when(has_down)(lambda: wait_recv(up_east, up_west))
        pl.when(has_up)(lambda: wait_recv(down_east, down_west))
        wait_recv(*wide)
        close()

    @pl.when(jnp.logical_not(polar))
    def _():
        wait_recv(*thin)
        for t in range(TILES):
            plain(t)

    pl.when(polar)(lambda: wait_send(*wide))
    pl.when(jnp.logical_not(polar))(lambda: wait_send(*thin))
    pl.when(has_up)(lambda: wait_send(up))
    pl.when(has_down)(lambda: wait_send(down))
    pl.when(to_up)(lambda: wait_send(up_east, up_west))
    pl.when(to_down)(lambda: wait_send(down_east, down_west))


def local(
    state, zonal_coef, diffusivity, coupling, filter_rows, band_width, table_index, coef_table
):
    turned = jnp.transpose(state, (1, 0, 2))
    args = (
        turned, zonal_coef[None, :], diffusivity[None, :], coupling,
        filter_rows[None, :], band_width[None, :], table_index[None, :], coef_table,
    )
    updated = pl.pallas_call(
        kernel,
        out_shape=pltpu.VMEM((COLS, ROWS, CH), F32),
        in_specs=[pl.BlockSpec(memory_space=pl.ANY)] * len(args),
        out_specs=pl.BlockSpec(memory_space=pltpu.VMEM),
        scratch_shapes=[
            pltpu.VMEM((COLS + 2 * HALO, ROWS + 16, CH), F32),
            pltpu.VMEM((TILES, COLS + 2 * MAXB, 8, CH), F32),
            pltpu.VMEM((MAXB + 1, TILES, 8, CH), F32),
            pltpu.VMEM((ROWS, CH), F32),
            pltpu.VMEM((ROWS, CH), F32),
            pltpu.VMEM((2 * CH, 2 * CH), BF16),
        ]
        + [pltpu.VMEM(a.shape, a.dtype) for a in args[1:]]
        + [
            pltpu.SemaphoreType.DMA((14,)),
            pltpu.SemaphoreType.DMA((14,)),
            pltpu.SemaphoreType.DMA((8,)),
            pltpu.SemaphoreType.REGULAR,
            pltpu.SemaphoreType.REGULAR,
            pltpu.SemaphoreType.REGULAR,
        ],
        compiler_params=pltpu.CompilerParams(
            collective_id=0, has_side_effects=True, vmem_limit_bytes=56 * 1024 * 1024
        ),
    )(*args)
    return jnp.transpose(updated, (1, 0, 2))


def solution(mesh):
    return jax.shard_map(
        local,
        mesh=mesh,
        in_specs=(P("lat", "lon", None), P("lat"), P(), P(), P(), P(), P(), P()),
        out_specs=P("lat", "lon", None),
        check_vma=False,
    )
```

```python
import jax
import jax.numpy as jnp
from jax import lax
from jax.experimental import pallas as pl
from jax.experimental.pallas import tpu as pltpu
from jax.sharding import PartitionSpec as P

MAXB = 16
HALO = MAXB + 1
MERIDIONAL = 0.1
ROWS = 32
COLS = 225
CH = 128
TILES = ROWS // 8
CHUNK = COLS - 2
PLAIN = 75
BLOCK = 8
MESH = pl.DeviceIdType.MESH
F32 = jnp.float32
BF16 = jnp.bfloat16


def chunks(total, size):
    return [min(i * size, total - size) for i in range((total + size - 1) // size)]


def kernel(
    st, zc, df, cp, fr, bw, ti, ct, out,
    S, C, W, A, C0, R, zc_v, df_v, cp_v, fr_v, bw_v, ti_v, ct_v, ss, rs, ls,
    from_east, from_west, from_lat,
):
    la = lax.axis_index("lat")
    lo = lax.axis_index("lon")
    east = lax.rem(lo + 1, 16)
    west = lax.rem(lo + 15, 16)

    def is_polar(pos):
        return (pos < 4) | (pos >= 12)

    polar = is_polar(la)
    has_up = la < 15
    has_down = la > 0

    barrier = pltpu.get_barrier_semaphore()

    place = lax.rem(lo, 8)
    first = place == 0
    pivot = place == 6
    final = place == 7
    rising = place < 6
    inside = jnp.logical_not(first | final)
    beside = jnp.where(has_up, 1, 0) + jnp.where(has_down, 1, 0)
    neighbours = 1 + beside

    def tell(semaphore, side):
        def one(device):
            pl.semaphore_signal(semaphore, inc=1, device_id=device, device_id_type=MESH)

        one((la, side))
        pl.when(has_up)(lambda: one((la + 1, side)))
        pl.when(has_down)(lambda: one((la - 1, side)))

    def tell_lat(semaphore):
        def one(device):
            pl.semaphore_signal(semaphore, inc=1, device_id=device, device_id_type=MESH)

        pl.when(has_up)(lambda: one((la + 1, lo)))
        pl.when(has_down)(lambda: one((la - 1, lo)))

    odd = lax.rem(la, 2) == 1
    even = jnp.logical_not(odd)
    pl.when(odd & jnp.logical_not(final))(lambda: tell_lat(barrier))
    pl.when(rising)(lambda: tell(barrier, east))
    pl.when(first)(lambda: tell(barrier, west))

    small = [(zc, zc_v), (df, df_v), (cp, cp_v), (fr, fr_v), (bw, bw_v), (ti, ti_v), (ct, ct_v)]
    loads = [pltpu.make_async_copy(src, dst, ls.at[i]) for i, (src, dst) in enumerate(small)]
    body = pltpu.make_async_copy(st, S.at[HALO : HALO + COLS, 8 : 8 + ROWS], ls.at[7])

    def fetch():
        body.start()
        for load in loads:
            load.start()

    pl.when(first)(fetch)

    def prepare():
        for load in loads:
            load.wait()
        body.wait()

        def iota(shape, dim):
            return lax.broadcasted_iota(jnp.int32, shape, dim)

        def column(values, offset):
            width = values.shape[1]
            pick = iota((ROWS, width), 1) == iota((ROWS, width), 0) + offset
            return jnp.sum(jnp.where(pick, values.astype(F32), 0.0), axis=1, keepdims=True)

        zonal = column(zc_v[...], 0)
        spread = df_v[...]
        A[...] = zonal * spread
        C0[...] = 1.0 - 2.0 * (zonal + MERIDIONAL) * spread
        fine = cp_v[...]
        coarse = fine.astype(BF16)
        rest = (fine - coarse.astype(F32)).astype(BF16)
        both = jnp.concatenate([coarse, rest], axis=1)
        R[...] = jnp.concatenate([both, both], axis=0)

        @pl.when(polar)
        def _():
            first = la * ROWS
            tables = column(ti_v[...], first)
            widths = column(bw_v[...], first)
            same = fr_v[...] == iota((ROWS, fr_v.shape[1]), 0) + first
            listed = jnp.sum(jnp.where(same, 1.0, 0.0), axis=1, keepdims=True) > 0.5
            taps = ct_v.shape[1]
            picked = jnp.zeros((ROWS, taps), F32)
            for table in range(ct_v.shape[0]):
                picked = jnp.where(tables == float(table), ct_v[table : table + 1, :], picked)
            reach = iota((ROWS, taps), 1)
            picked = jnp.where(reach.astype(F32) <= widths, picked, 0.0)
            picked = jnp.where(listed, picked, jnp.where(reach == 0, 1.0, 0.0))
            for k in range(taps):
                W[k] = jnp.broadcast_to(picked[:, k : k + 1], (ROWS, CH)).reshape(TILES, 8, CH)

    def stepped(t, q0, size):
        low = 8 + 8 * t
        centre = S[pl.ds(q0 + 1, size), low : low + 8, :]
        sides = S[pl.ds(q0 + 2, size), low : low + 8, :] + S[pl.ds(q0, size), low : low + 8, :]
        poles = (
            S[pl.ds(q0 + 1, size), low + 1 : low + 9, :]
            + S[pl.ds(q0 + 1, size), low - 1 : low + 7, :]
        )
        rows = slice(8 * t, 8 * t + 8)
        value = (
            C0[rows][None] * centre
            + A[rows][None] * sides
            + (MERIDIONAL * df_v[...])[None] * poles
        )
        return value.reshape(size * 8, CH)

    def couple(*parts):
        flat = [stepped(*part) for part in parts]
        flat = flat[0] if len(flat) == 1 else jnp.concatenate(flat, axis=0)
        big = flat.astype(BF16)
        small = (flat - big.astype(F32)).astype(BF16)
        wide = jnp.dot(
            jnp.concatenate([big, small], axis=1), R[...], preferred_element_type=F32
        )
        flat = flat + (wide[:, :CH] + wide[:, CH:])
        return flat.reshape(flat.shape[0] // 8, 8, CH)

    def smooth(t, i0, size):
        window = [C[t, i0 + m] for m in range(size + 2 * MAXB)]
        total = [W[0, t] * window[b + MAXB] for b in range(size)]
        for k in range(1, MAXB + 1):
            weight = W[k, t]
            for b in range(size):
                total[b] = total[b] + weight * (window[b + MAXB - k] + window[b + MAXB + k])
        for b in range(size):
            out[i0 + b, pl.ds(pl.multiple_of(8 * t, 8), 8), :] = total[b]

    def inner(t):
        n = COLS - 2
        steps = (n + CHUNK - 1) // CHUNK

        @pl.loop(0, steps)
        def _(j):
            q0 = HALO + jnp.minimum(j * CHUNK, n - CHUNK)
            C[t, pl.ds(q0, CHUNK)] = couple((t, q0, CHUNK))

        m = COLS - 2 * HALO
        steps = (m + BLOCK - 1) // BLOCK

        @pl.loop(0, steps)
        def _(j):
            smooth(t, HALO + jnp.minimum(j * BLOCK, m - BLOCK), BLOCK)

    def edge(t, right, known):
        place = [COLS - 1 - i if right else i for i in range(HALO)]
        rows = pl.ds(pl.multiple_of(8 * t, 8), 8)
        most = HALO + 2 * MAXB
        wanted = range(HALO, most) if known else range(HALO)
        source = {q: C[t, COLS + 2 * MAXB - 1 - q if right else q] for q in wanted}
        total = [None if known else out[i, rows, :] for i in place]
        for k in range(MAXB + 1):
            weight = W[k, t]
            for i in range(HALO):
                reached = sorted({i + MAXB - k, i + MAXB + k})
                values = [source[q] for q in reached if q in source]
                if values:
                    value = weight * (values[0] if len(values) == 1 else values[0] + values[1])
                    total[i] = value if total[i] is None else total[i] + value
        for i in range(HALO):
            out[place[i], rows, :] = total[i]

    def both_edges(known):
        @pl.loop(0, TILES)
        def _(t):
            edge(t, False, known)
            edge(t, True, known)

    def close():
        far = COLS + MAXB - 1
        parts = [(t, q0, HALO) for t in range(TILES) for q0 in (0, far)]
        value = couple(*parts)
        for i, (t, q0, size) in enumerate(parts):
            C[t, q0 : q0 + size] = value[i * size : i * size + size]
        both_edges(False)

    def plain(t):
        @pl.loop(0, COLS // PLAIN)
        def _(j):
            i0 = j * PLAIN
            out[pl.ds(i0, PLAIN), 8 * t : 8 * t + 8, :] = couple((t, i0 + MAXB, PLAIN))

    count = (
        jnp.where(odd | final, 0, beside)
        + jnp.where(inside, neighbours, 0)
        + jnp.where(pivot | final, neighbours, 0)
    )
    pl.when(count > 0)(lambda: pl.semaphore_wait(barrier, count))

    def send(src, dst, i, device):
        return pltpu.make_async_remote_copy(
            src_ref=src, dst_ref=dst, send_sem=ss.at[i], recv_sem=rs.at[i],
            device_id=device, device_id_type=MESH,
        )

    last = COLS - HALO
    high = HALO + COLS
    wide = (
        send(st.at[last:COLS], S.at[0:HALO, 8 : 8 + ROWS], 2, (la, east)),
        send(st.at[0:HALO], S.at[high : high + HALO, 8 : 8 + ROWS], 3, (la, west)),
    )
    thin = (
        send(st.at[COLS - 1 : COLS], S.at[HALO - 1 : HALO, 8 : 8 + ROWS], 0, (la, east)),
        send(st.at[0:1], S.at[high : high + 1, 8 : 8 + ROWS], 1, (la, west)),
    )
    up = send(st.at[:, 31:32], S.at[HALO:high, 7:8], 8, (la + 1, lo))
    down = send(st.at[:, 0:1], S.at[HALO:high, 40:41], 9, (la - 1, lo))
    up_east = send(st.at[last:COLS, 31:32], S.at[0:HALO, 7:8], 10, (la + 1, east))
    up_west = send(st.at[0:HALO, 31:32], S.at[high : high + HALO, 7:8], 11, (la + 1, west))
    down_east = send(st.at[last:COLS, 0:1], S.at[0:HALO, 40:41], 12, (la - 1, east))
    down_west = send(st.at[0:HALO, 0:1], S.at[high : high + HALO, 40:41], 13, (la - 1, west))

    def start(*copies):
        for copy in copies:
            copy.start()

    def wait_send(*copies):
        for copy in copies:
            copy.wait_send()

    def wait_recv(*copies):
        for copy in copies:
            copy.wait_recv()

    to_up = has_up & is_polar(la + 1)
    to_down = has_down & is_polar(la - 1)

    def start_east():
        pl.when(to_up)(lambda: start(up_east))
        pl.when(to_down)(lambda: start(down_east))
        pl.when(polar)(lambda: start(wide[0]))
        pl.when(jnp.logical_not(polar))(lambda: start(thin[0]))

    def start_west():
        pl.when(to_up)(lambda: start(up_west))
        pl.when(to_down)(lambda: start(down_west))
        pl.when(polar)(lambda: start(wide[1]))
        pl.when(jnp.logical_not(polar))(lambda: start(thin[1]))

    def start_lat():
        pl.when(has_up)(lambda: start(up))
        pl.when(has_down)(lambda: start(down))

    @pl.when(final)
    def _():
        tell(from_west, east)
        start_east()
        tell(barrier, west)

    @pl.when(inside)
    def _():
        tell(from_east, west)
        pl.when(pivot)(lambda: tell(from_west, east))
        start_west()

    pl.when(even & jnp.logical_not(final))(lambda: tell_lat(from_lat))
    pl.when(pivot)(start_east)
    pl.when(jnp.logical_not(first))(fetch)
    pl.when(even & jnp.logical_not(final))(start_lat)

    @pl.when(rising)
    def _():
        pl.semaphore_wait(from_east, neighbours)
        start_east()

    @pl.when(odd & jnp.logical_not(final))
    def _():
        pl.semaphore_wait(from_lat, beside)
        start_lat()

    @pl.when(final)
    def _():
        pl.semaphore_wait(from_west, neighbours)
        start_west()

    def answer():
        pl.semaphore_wait(from_west, neighbours)
        pl.semaphore_signal(from_lat, inc=1, device_id=(la, west), device_id_type=MESH)
        start_west()

    def follow():
        pl.semaphore_wait(from_lat, 1)
        start_lat()

    def clear(row):
        S[:, row : row + 1, :] = jnp.zeros((S.shape[0], 1, CH), F32)

    pl.when(jnp.logical_not(has_down))(lambda: clear(7))
    pl.when(jnp.logical_not(has_up))(lambda: clear(40))

    prepare()
    pl.when(polar)(lambda: inner(1))
    pl.when(final)(follow)
    pl.when(lo == 8)(answer)
    pl.when(polar)(lambda: inner(2))
    pl.when(lo == 0)(answer)
    pl.when(has_down)(lambda: wait_recv(up))
    pl.when(has_up)(lambda: wait_recv(down))

    @pl.when(polar)
    def _():
        inner(0)
        inner(3)
        both_edges(True)
        pl.when(has_down)(lambda: wait_recv(up_east, up_west))
        pl.when(has_up)(lambda: wait_recv(down_east, down_west))
        wait_recv(*wide)
        close()

    @pl.when(jnp.logical_not(polar))
    def _():
        wait_recv(*thin)
        for t in range(TILES):
            plain(t)

    pl.when(polar)(lambda: wait_send(*wide))
    pl.when(jnp.logical_not(polar))(lambda: wait_send(*thin))
    pl.when(has_up)(lambda: wait_send(up))
    pl.when(has_down)(lambda: wait_send(down))
    pl.when(to_up)(lambda: wait_send(up_east, up_west))
    pl.when(to_down)(lambda: wait_send(down_east, down_west))


def local(
    state, zonal_coef, diffusivity, coupling, filter_rows, band_width, table_index, coef_table
):
    turned = jnp.transpose(state, (1, 0, 2))
    args = (
        turned, zonal_coef[None, :], diffusivity[None, :], coupling,
        filter_rows[None, :], band_width[None, :], table_index[None, :], coef_table,
    )
    updated = pl.pallas_call(
        kernel,
        out_shape=pltpu.VMEM((COLS, ROWS, CH), F32),
        in_specs=[pl.BlockSpec(memory_space=pl.ANY)] * len(args),
        out_specs=pl.BlockSpec(memory_space=pltpu.VMEM),
        scratch_shapes=[
            pltpu.VMEM((COLS + 2 * HALO, ROWS + 16, CH), F32),
            pltpu.VMEM((TILES, COLS + 2 * MAXB, 8, CH), F32),
            pltpu.VMEM((MAXB + 1, TILES, 8, CH), F32),
            pltpu.VMEM((ROWS, CH), F32),
            pltpu.VMEM((ROWS, CH), F32),
            pltpu.VMEM((2 * CH, 2 * CH), BF16),
        ]
        + [pltpu.VMEM(a.shape, a.dtype) for a in args[1:]]
        + [
            pltpu.SemaphoreType.DMA((14,)),
            pltpu.SemaphoreType.DMA((14,)),
            pltpu.SemaphoreType.DMA((8,)),
            pltpu.SemaphoreType.REGULAR,
            pltpu.SemaphoreType.REGULAR,
            pltpu.SemaphoreType.REGULAR,
        ],
        compiler_params=pltpu.CompilerParams(
            collective_id=0, has_side_effects=True, vmem_limit_bytes=56 * 1024 * 1024
        ),
    )(*args)
    return jnp.transpose(updated, (1, 0, 2))


def solution(mesh):
    return jax.shard_map(
        local,
        mesh=mesh,
        in_specs=(P("lat", "lon", None), P("lat"), P(), P(), P(), P(), P(), P()),
        out_specs=P("lat", "lon", None),
        check_vma=False,
    )
```

```python
import jax
import jax.numpy as jnp
from jax import lax
from jax.experimental import pallas as pl
from jax.experimental.pallas import tpu as pltpu
from jax.sharding import PartitionSpec as P

MAXB = 16
HALO = MAXB + 1
MERIDIONAL = 0.1
ROWS = 32
COLS = 225
CH = 128
TILES = ROWS // 8
CHUNK = COLS - 2
PLAIN = 75
BLOCK = 8
MESH = pl.DeviceIdType.MESH
F32 = jnp.float32
BF16 = jnp.bfloat16


def chunks(total, size):
    return [min(i * size, total - size) for i in range((total + size - 1) // size)]


def kernel(
    st, zc, df, cp, fr, bw, ti, ct, out,
    S, C, W, A, C0, R, zc_v, df_v, cp_v, fr_v, bw_v, ti_v, ct_v, ss, rs, ls,
    from_east, from_west, from_lat,
):
    la = lax.axis_index("lat")
    lo = lax.axis_index("lon")
    east = lax.rem(lo + 1, 16)
    west = lax.rem(lo + 15, 16)

    def is_polar(pos):
        return (pos < 4) | (pos >= 12)

    polar = is_polar(la)
    has_up = la < 15
    has_down = la > 0

    barrier = pltpu.get_barrier_semaphore()

    place = lax.rem(lo, 8)
    first = place == 0
    pivot = place == 6
    final = place == 7
    rising = place < 6
    inside = jnp.logical_not(first | final)
    beside = jnp.where(has_up, 1, 0) + jnp.where(has_down, 1, 0)
    neighbours = 1 + beside

    def tell(semaphore, side):
        def one(device):
            pl.semaphore_signal(semaphore, inc=1, device_id=device, device_id_type=MESH)

        one((la, side))
        pl.when(has_up)(lambda: one((la + 1, side)))
        pl.when(has_down)(lambda: one((la - 1, side)))

    def tell_lat(semaphore):
        def one(device):
            pl.semaphore_signal(semaphore, inc=1, device_id=device, device_id_type=MESH)

        pl.when(has_up)(lambda: one((la + 1, lo)))
        pl.when(has_down)(lambda: one((la - 1, lo)))

    odd = lax.rem(la, 2) == 1
    even = jnp.logical_not(odd)
    pl.when(odd & jnp.logical_not(final))(lambda: tell_lat(barrier))
    pl.when(rising)(lambda: tell(barrier, east))
    pl.when(first)(lambda: tell(barrier, west))

    small = [(zc, zc_v), (df, df_v), (cp, cp_v), (fr, fr_v), (bw, bw_v), (ti, ti_v), (ct, ct_v)]
    loads = [pltpu.make_async_copy(src, dst, ls.at[i]) for i, (src, dst) in enumerate(small)]
    body = pltpu.make_async_copy(st, S.at[HALO : HALO + COLS, 8 : 8 + ROWS], ls.at[7])

    def fetch():
        for load in loads:
            load.start()
        body.start()

    pl.when(first)(fetch)

    def prepare():
        for load in loads:
            load.wait()

        def iota(shape, dim):
            return lax.broadcasted_iota(jnp.int32, shape, dim)

        def column(values, offset):
            width = values.shape[1]
            pick = iota((ROWS, width), 1) == iota((ROWS, width), 0) + offset
            return jnp.sum(jnp.where(pick, values.astype(F32), 0.0), axis=1, keepdims=True)

        zonal = column(zc_v[...], 0)
        spread = df_v[...]
        A[...] = zonal * spread
        C0[...] = 1.0 - 2.0 * (zonal + MERIDIONAL) * spread
        fine = cp_v[...]
        coarse = fine.astype(BF16)
        rest = (fine - coarse.astype(F32)).astype(BF16)
        both = jnp.concatenate([coarse, rest], axis=1)
        R[...] = jnp.concatenate([both, both], axis=0)

        @pl.when(polar)
        def _():
            first = la * ROWS
            tables = column(ti_v[...], first)
            widths = column(bw_v[...], first)
            same = fr_v[...] == iota((ROWS, fr_v.shape[1]), 0) + first
            listed = jnp.sum(jnp.where(same, 1.0, 0.0), axis=1, keepdims=True) > 0.5
            taps = ct_v.shape[1]
            picked = jnp.zeros((ROWS, taps), F32)
            for table in range(ct_v.shape[0]):
                picked = jnp.where(tables == float(table), ct_v[table : table + 1, :], picked)
            reach = iota((ROWS, taps), 1)
            picked = jnp.where(reach.astype(F32) <= widths, picked, 0.0)
            picked = jnp.where(listed, picked, jnp.where(reach == 0, 1.0, 0.0))
            for k in range(taps):
                W[k] = jnp.broadcast_to(picked[:, k : k + 1], (ROWS, CH)).reshape(TILES, 8, CH)

    def stepped(t, q0, size):
        low = 8 + 8 * t
        centre = S[pl.ds(q0 + 1, size), low : low + 8, :]
        sides = S[pl.ds(q0 + 2, size), low : low + 8, :] + S[pl.ds(q0, size), low : low + 8, :]
        poles = (
            S[pl.ds(q0 + 1, size), low + 1 : low + 9, :]
            + S[pl.ds(q0 + 1, size), low - 1 : low + 7, :]
        )
        rows = slice(8 * t, 8 * t + 8)
        value = (
            C0[rows][None] * centre
            + A[rows][None] * sides
            + (MERIDIONAL * df_v[...])[None] * poles
        )
        return value.reshape(size * 8, CH)

    def couple(*parts):
        flat = [stepped(*part) for part in parts]
        flat = flat[0] if len(flat) == 1 else jnp.concatenate(flat, axis=0)
        big = flat.astype(BF16)
        small = (flat - big.astype(F32)).astype(BF16)
        wide = jnp.dot(
            jnp.concatenate([big, small], axis=1), R[...], preferred_element_type=F32
        )
        flat = flat + (wide[:, :CH] + wide[:, CH:])
        return flat.reshape(flat.shape[0] // 8, 8, CH)

    def smooth(t, i0, size):
        window = [C[t, i0 + m] for m in range(size + 2 * MAXB)]
        total = [W[0, t] * window[b + MAXB] for b in range(size)]
        for k in range(1, MAXB + 1):
            weight = W[k, t]
            for b in range(size):
                total[b] = total[b] + weight * (window[b + MAXB - k] + window[b + MAXB + k])
        for b in range(size):
            out[i0 + b, pl.ds(pl.multiple_of(8 * t, 8), 8), :] = total[b]

    def inner(t):
        n = COLS - 2
        steps = (n + CHUNK - 1) // CHUNK

        @pl.loop(0, steps)
        def _(j):
            q0 = HALO + jnp.minimum(j * CHUNK, n - CHUNK)
            C[t, pl.ds(q0, CHUNK)] = couple((t, q0, CHUNK))

        m = COLS - 2 * HALO
        steps = (m + BLOCK - 1) // BLOCK

        @pl.loop(0, steps)
        def _(j):
            smooth(t, HALO + jnp.minimum(j * BLOCK, m - BLOCK), BLOCK)

    def edge(t, right, known):
        place = [COLS - 1 - i if right else i for i in range(HALO)]
        rows = pl.ds(pl.multiple_of(8 * t, 8), 8)
        most = HALO + 2 * MAXB
        wanted = range(HALO, most) if known else range(HALO)
        source = {q: C[t, COLS + 2 * MAXB - 1 - q if right else q] for q in wanted}
        total = [None if known else out[i, rows, :] for i in place]
        for k in range(MAXB + 1):
            weight = W[k, t]
            for i in range(HALO):
                reached = sorted({i + MAXB - k, i + MAXB + k})
                values = [source[q] for q in reached if q in source]
                if values:
                    value = weight * (values[0] if len(values) == 1 else values[0] + values[1])
                    total[i] = value if total[i] is None else total[i] + value
        for i in range(HALO):
            out[place[i], rows, :] = total[i]

    def both_edges(known):
        @pl.loop(0, TILES)
        def _(t):
            edge(t, False, known)
            edge(t, True, known)

    def close():
        far = COLS + MAXB - 1
        parts = [(t, q0, HALO) for t in range(TILES) for q0 in (0, far)]
        value = couple(*parts)
        for i, (t, q0, size) in enumerate(parts):
            C[t, q0 : q0 + size] = value[i * size : i * size + size]
        both_edges(False)

    def plain(t):
        @pl.loop(0, COLS // PLAIN)
        def _(j):
            i0 = j * PLAIN
            out[pl.ds(i0, PLAIN), 8 * t : 8 * t + 8, :] = couple((t, i0 + MAXB, PLAIN))

    count = (
        jnp.where(odd | final, 0, beside)
        + jnp.where(inside, neighbours, 0)
        + jnp.where(pivot | final, neighbours, 0)
    )
    pl.when(count > 0)(lambda: pl.semaphore_wait(barrier, count))

    def send(src, dst, i, device):
        return pltpu.make_async_remote_copy(
            src_ref=src, dst_ref=dst, send_sem=ss.at[i], recv_sem=rs.at[i],
            device_id=device, device_id_type=MESH,
        )

    last = COLS - HALO
    high = HALO + COLS
    wide = (
        send(st.at[last:COLS], S.at[0:HALO, 8 : 8 + ROWS], 2, (la, east)),
        send(st.at[0:HALO], S.at[high : high + HALO, 8 : 8 + ROWS], 3, (la, west)),
    )
    thin = (
        send(st.at[COLS - 1 : COLS], S.at[HALO - 1 : HALO, 8 : 8 + ROWS], 0, (la, east)),
        send(st.at[0:1], S.at[high : high + 1, 8 : 8 + ROWS], 1, (la, west)),
    )
    up = send(st.at[:, 31:32], S.at[HALO:high, 7:8], 8, (la + 1, lo))
    down = send(st.at[:, 0:1], S.at[HALO:high, 40:41], 9, (la - 1, lo))
    up_east = send(st.at[last:COLS, 31:32], S.at[0:HALO, 7:8], 10, (la + 1, east))
    up_west = send(st.at[0:HALO, 31:32], S.at[high : high + HALO, 7:8], 11, (la + 1, west))
    down_east = send(st.at[last:COLS, 0:1], S.at[0:HALO, 40:41], 12, (la - 1, east))
    down_west = send(st.at[0:HALO, 0:1], S.at[high : high + HALO, 40:41], 13, (la - 1, west))

    def start(*copies):
        for copy in copies:
            copy.start()

    def wait_send(*copies):
        for copy in copies:
            copy.wait_send()

    def wait_recv(*copies):
        for copy in copies:
            copy.wait_recv()

    to_up = has_up & is_polar(la + 1)
    to_down = has_down & is_polar(la - 1)

    def start_east():
        pl.when(to_up)(lambda: start(up_east))
        pl.when(to_down)(lambda: start(down_east))
        pl.when(polar)(lambda: start(wide[0]))
        pl.when(jnp.logical_not(polar))(lambda: start(thin[0]))

    def start_west():
        pl.when(to_up)(lambda: start(up_west))
        pl.when(to_down)(lambda: start(down_west))
        pl.when(polar)(lambda: start(wide[1]))
        pl.when(jnp.logical_not(polar))(lambda: start(thin[1]))

    def start_lat():
        pl.when(has_up)(lambda: start(up))
        pl.when(has_down)(lambda: start(down))

    @pl.when(final)
    def _():
        tell(from_west, east)
        start_east()
        tell(barrier, west)

    pl.when(even & jnp.logical_not(final))(lambda: tell_lat(from_lat))

    @pl.when(inside)
    def _():
        pl.when(pivot)(lambda: tell(from_west, east))
        tell(from_east, west)

    pl.when(even & jnp.logical_not(final))(start_lat)
    pl.when(inside)(start_west)
    pl.when(pivot)(start_east)
    pl.when(jnp.logical_not(first))(fetch)

    prepare()
    body.wait()

    @pl.when(odd & jnp.logical_not(final))
    def _():
        pl.semaphore_wait(from_lat, beside)
        start_lat()

    @pl.when(rising)
    def _():
        pl.semaphore_wait(from_east, neighbours)
        start_east()

    @pl.when(final)
    def _():
        pl.semaphore_wait(from_west, neighbours)
        start_lat()
        start_west()

    def answer():
        pl.semaphore_wait(from_west, neighbours)
        start_west()

    def clear(row):
        S[:, row : row + 1, :] = jnp.zeros((S.shape[0], 1, CH), F32)

    pl.when(jnp.logical_not(has_down))(lambda: clear(7))
    pl.when(jnp.logical_not(has_up))(lambda: clear(40))

    pl.when(polar)(lambda: inner(1))
    pl.when(lo == 8)(answer)
    pl.when(polar)(lambda: inner(2))
    pl.when(lo == 0)(answer)
    pl.when(has_down)(lambda: wait_recv(up))
    pl.when(has_up)(lambda: wait_recv(down))

    @pl.when(polar)
    def _():
        inner(0)
        inner(3)
        both_edges(True)
        pl.when(has_down)(lambda: wait_recv(up_east, up_west))
        pl.when(has_up)(lambda: wait_recv(down_east, down_west))
        wait_recv(*wide)
        close()

    @pl.when(jnp.logical_not(polar))
    def _():
        wait_recv(*thin)
        for t in range(TILES):
            plain(t)

    pl.when(polar)(lambda: wait_send(*wide))
    pl.when(jnp.logical_not(polar))(lambda: wait_send(*thin))
    pl.when(has_up)(lambda: wait_send(up))
    pl.when(has_down)(lambda: wait_send(down))
    pl.when(to_up)(lambda: wait_send(up_east, up_west))
    pl.when(to_down)(lambda: wait_send(down_east, down_west))


def local(
    state, zonal_coef, diffusivity, coupling, filter_rows, band_width, table_index, coef_table
):
    turned = jnp.transpose(state, (1, 0, 2))
    args = (
        turned, zonal_coef[None, :], diffusivity[None, :], coupling,
        filter_rows[None, :], band_width[None, :], table_index[None, :], coef_table,
    )
    updated = pl.pallas_call(
        kernel,
        out_shape=pltpu.VMEM((COLS, ROWS, CH), F32),
        in_specs=[pl.BlockSpec(memory_space=pl.ANY)] * len(args),
        out_specs=pl.BlockSpec(memory_space=pltpu.VMEM),
        scratch_shapes=[
            pltpu.VMEM((COLS + 2 * HALO, ROWS + 16, CH), F32),
            pltpu.VMEM((TILES, COLS + 2 * MAXB, 8, CH), F32),
            pltpu.VMEM((MAXB + 1, TILES, 8, CH), F32),
            pltpu.VMEM((ROWS, CH), F32),
            pltpu.VMEM((ROWS, CH), F32),
            pltpu.VMEM((2 * CH, 2 * CH), BF16),
        ]
        + [pltpu.VMEM(a.shape, a.dtype) for a in args[1:]]
        + [
            pltpu.SemaphoreType.DMA((14,)),
            pltpu.SemaphoreType.DMA((14,)),
            pltpu.SemaphoreType.DMA((8,)),
            pltpu.SemaphoreType.REGULAR,
            pltpu.SemaphoreType.REGULAR,
            pltpu.SemaphoreType.REGULAR,
        ],
        compiler_params=pltpu.CompilerParams(
            collective_id=0, has_side_effects=True, vmem_limit_bytes=56 * 1024 * 1024
        ),
    )(*args)
    return jnp.transpose(updated, (1, 0, 2))


def solution(mesh):
    return jax.shard_map(
        local,
        mesh=mesh,
        in_specs=(P("lat", "lon", None), P("lat"), P(), P(), P(), P(), P(), P()),
        out_specs=P("lat", "lon", None),
        check_vma=False,
    )
```

```python
import jax
import jax.numpy as jnp
from jax import lax
from jax.experimental import pallas as pl
from jax.experimental.pallas import tpu as pltpu
from jax.sharding import PartitionSpec as P

MAXB = 16
HALO = MAXB + 1
MERIDIONAL = 0.1
ROWS = 32
COLS = 225
CH = 128
TILES = ROWS // 8
CHUNK = COLS - 2
PLAIN = 75
BLOCK = 8
MESH = pl.DeviceIdType.MESH
F32 = jnp.float32
BF16 = jnp.bfloat16


def chunks(total, size):
    return [min(i * size, total - size) for i in range((total + size - 1) // size)]


def kernel(
    st, zc, df, cp, fr, bw, ti, ct, out,
    S, C, W, A, C0, R, zc_v, df_v, cp_v, fr_v, bw_v, ti_v, ct_v, ss, rs, ls,
    from_east, from_west, from_far, from_lat,
):
    la = lax.axis_index("lat")
    lo = lax.axis_index("lon")
    east = lax.rem(lo + 1, 16)
    west = lax.rem(lo + 15, 16)

    def is_polar(pos):
        return (pos < 4) | (pos >= 12)

    polar = is_polar(la)
    has_up = la < 15
    has_down = la > 0

    barrier = pltpu.get_barrier_semaphore()

    place = lax.rem(lo, 8)
    first = place == 0
    pivot = place == 6
    final = place == 7
    rising = place < 6
    inside = jnp.logical_not(first | final)
    beside = jnp.where(has_up, 1, 0) + jnp.where(has_down, 1, 0)
    neighbours = 1 + beside

    def tell_one(semaphore, device):
        pl.semaphore_signal(semaphore, inc=1, device_id=device, device_id_type=MESH)

    def tell_far(semaphore, side):
        pl.when(has_up)(lambda: tell_one(semaphore, (la + 1, side)))
        pl.when(has_down)(lambda: tell_one(semaphore, (la - 1, side)))

    def tell(semaphore, side):
        tell_one(semaphore, (la, side))
        tell_far(semaphore, side)

    def tell_lat(semaphore):
        tell_far(semaphore, lo)

    odd = lax.rem(la, 2) == 1
    even = jnp.logical_not(odd)
    pl.when(odd & jnp.logical_not(final))(lambda: tell_lat(barrier))
    pl.when(rising)(lambda: tell(barrier, east))
    pl.when(first)(lambda: tell(barrier, west))

    small = [(zc, zc_v), (df, df_v), (cp, cp_v), (fr, fr_v), (bw, bw_v), (ti, ti_v), (ct, ct_v)]
    loads = [pltpu.make_async_copy(src, dst, ls.at[i]) for i, (src, dst) in enumerate(small)]
    body = pltpu.make_async_copy(st, S.at[HALO : HALO + COLS, 8 : 8 + ROWS], ls.at[7])

    def fetch():
        for load in loads:
            load.start()
        body.start()

    pl.when(first)(fetch)

    def prepare():
        for load in loads:
            load.wait()

        def iota(shape, dim):
            return lax.broadcasted_iota(jnp.int32, shape, dim)

        def column(values, offset):
            width = values.shape[1]
            pick = iota((ROWS, width), 1) == iota((ROWS, width), 0) + offset
            return jnp.sum(jnp.where(pick, values.astype(F32), 0.0), axis=1, keepdims=True)

        zonal = column(zc_v[...], 0)
        spread = df_v[...]
        A[...] = zonal * spread
        C0[...] = 1.0 - 2.0 * (zonal + MERIDIONAL) * spread
        fine = cp_v[...]
        coarse = fine.astype(BF16)
        rest = (fine - coarse.astype(F32)).astype(BF16)
        both = jnp.concatenate([coarse, rest], axis=1)
        R[...] = jnp.concatenate([both, both], axis=0)

        @pl.when(polar)
        def _():
            first = la * ROWS
            tables = column(ti_v[...], first)
            widths = column(bw_v[...], first)
            same = fr_v[...] == iota((ROWS, fr_v.shape[1]), 0) + first
            listed = jnp.sum(jnp.where(same, 1.0, 0.0), axis=1, keepdims=True) > 0.5
            taps = ct_v.shape[1]
            picked = jnp.zeros((ROWS, taps), F32)
            for table in range(ct_v.shape[0]):
                picked = jnp.where(tables == float(table), ct_v[table : table + 1, :], picked)
            reach = iota((ROWS, taps), 1)
            picked = jnp.where(reach.astype(F32) <= widths, picked, 0.0)
            picked = jnp.where(listed, picked, jnp.where(reach == 0, 1.0, 0.0))
            for k in range(taps):
                W[k] = jnp.broadcast_to(picked[:, k : k + 1], (ROWS, CH)).reshape(TILES, 8, CH)

    def stepped(t, q0, size):
        low = 8 + 8 * t
        centre = S[pl.ds(q0 + 1, size), low : low + 8, :]
        sides = S[pl.ds(q0 + 2, size), low : low + 8, :] + S[pl.ds(q0, size), low : low + 8, :]
        poles = (
            S[pl.ds(q0 + 1, size), low + 1 : low + 9, :]
            + S[pl.ds(q0 + 1, size), low - 1 : low + 7, :]
        )
        rows = slice(8 * t, 8 * t + 8)
        value = (
            C0[rows][None] * centre
            + A[rows][None] * sides
            + (MERIDIONAL * df_v[...])[None] * poles
        )
        return value.reshape(size * 8, CH)

    def couple(*parts):
        flat = [stepped(*part) for part in parts]
        flat = flat[0] if len(flat) == 1 else jnp.concatenate(flat, axis=0)
        big = flat.astype(BF16)
        small = (flat - big.astype(F32)).astype(BF16)
        wide = jnp.dot(
            jnp.concatenate([big, small], axis=1), R[...], preferred_element_type=F32
        )
        flat = flat + (wide[:, :CH] + wide[:, CH:])
        return flat.reshape(flat.shape[0] // 8, 8, CH)

    def smooth(t, i0, size):
        window = [C[t, i0 + m] for m in range(size + 2 * MAXB)]
        total = [W[0, t] * window[b + MAXB] for b in range(size)]
        for k in range(1, MAXB + 1):
            weight = W[k, t]
            for b in range(size):
                total[b] = total[b] + weight * (window[b + MAXB - k] + window[b + MAXB + k])
        for b in range(size):
            out[i0 + b, pl.ds(pl.multiple_of(8 * t, 8), 8), :] = total[b]

    def inner(t):
        n = COLS - 2
        steps = (n + CHUNK - 1) // CHUNK

        @pl.loop(0, steps)
        def _(j):
            q0 = HALO + jnp.minimum(j * CHUNK, n - CHUNK)
            C[t, pl.ds(q0, CHUNK)] = couple((t, q0, CHUNK))

        m = COLS - 2 * HALO
        steps = (m + BLOCK - 1) // BLOCK

        @pl.loop(0, steps)
        def _(j):
            smooth(t, HALO + jnp.minimum(j * BLOCK, m - BLOCK), BLOCK)

    def edge(t, right, known):
        place = [COLS - 1 - i if right else i for i in range(HALO)]
        rows = pl.ds(pl.multiple_of(8 * t, 8), 8)
        most = HALO + 2 * MAXB
        wanted = range(HALO, most) if known else range(HALO)
        source = {q: C[t, COLS + 2 * MAXB - 1 - q if right else q] for q in wanted}
        total = [None if known else out[i, rows, :] for i in place]
        for k in range(MAXB + 1):
            weight = W[k, t]
            for i in range(HALO):
                reached = sorted({i + MAXB - k, i + MAXB + k})
                values = [source[q] for q in reached if q in source]
                if values:
                    value = weight * (values[0] if len(values) == 1 else values[0] + values[1])
                    total[i] = value if total[i] is None else total[i] + value
        for i in range(HALO):
            out[place[i], rows, :] = total[i]

    def both_edges(known):
        @pl.loop(0, TILES)
        def _(t):
            edge(t, False, known)
            edge(t, True, known)

    def close(right):
        pl.when(has_down)(lambda: wait_recv(up_west if right else up_east))
        pl.when(has_up)(lambda: wait_recv(down_west if right else down_east))
        wait_recv(wide[1] if right else wide[0])
        q0 = COLS + MAXB - 1 if right else 0
        value = couple(*[(t, q0, HALO) for t in range(TILES)])
        for t in range(TILES):
            C[t, q0 : q0 + HALO] = value[t * HALO : t * HALO + HALO]

        @pl.loop(0, TILES)
        def _(t):
            edge(t, right, False)

    def plain(t):
        @pl.loop(0, COLS // PLAIN)
        def _(j):
            i0 = j * PLAIN
            out[pl.ds(i0, PLAIN), 8 * t : 8 * t + 8, :] = couple((t, i0 + MAXB, PLAIN))

    count = (
        jnp.where(odd | final, 0, beside)
        + jnp.where(inside, neighbours, 0)
        + jnp.where(pivot | final, neighbours, 0)
    )
    pl.when(count > 0)(lambda: pl.semaphore_wait(barrier, count))

    def send(src, dst, i, device):
        return pltpu.make_async_remote_copy(
            src_ref=src, dst_ref=dst, send_sem=ss.at[i], recv_sem=rs.at[i],
            device_id=device, device_id_type=MESH,
        )

    last = COLS - HALO
    high = HALO + COLS
    wide = (
        send(st.at[last:COLS], S.at[0:HALO, 8 : 8 + ROWS], 2, (la, east)),
        send(st.at[0:HALO], S.at[high : high + HALO, 8 : 8 + ROWS], 3, (la, west)),
    )
    thin = (
        send(st.at[COLS - 1 : COLS], S.at[HALO - 1 : HALO, 8 : 8 + ROWS], 0, (la, east)),
        send(st.at[0:1], S.at[high : high + 1, 8 : 8 + ROWS], 1, (la, west)),
    )
    up = send(st.at[:, 31:32], S.at[HALO:high, 7:8], 8, (la + 1, lo))
    down = send(st.at[:, 0:1], S.at[HALO:high, 40:41], 9, (la - 1, lo))
    up_east = send(st.at[last:COLS, 31:32], S.at[0:HALO, 7:8], 10, (la + 1, east))
    up_west = send(st.at[0:HALO, 31:32], S.at[high : high + HALO, 7:8], 11, (la + 1, west))
    down_east = send(st.at[last:COLS, 0:1], S.at[0:HALO, 40:41], 12, (la - 1, east))
    down_west = send(st.at[0:HALO, 0:1], S.at[high : high + HALO, 40:41], 13, (la - 1, west))

    def start(*copies):
        for copy in copies:
            copy.start()

    def wait_send(*copies):
        for copy in copies:
            copy.wait_send()

    def wait_recv(*copies):
        for copy in copies:
            copy.wait_recv()

    to_up = has_up & is_polar(la + 1)
    to_down = has_down & is_polar(la - 1)

    def start_east():
        pl.when(to_up)(lambda: start(up_east))
        pl.when(to_down)(lambda: start(down_east))
        pl.when(polar)(lambda: start(wide[0]))
        pl.when(jnp.logical_not(polar))(lambda: start(thin[0]))

    def start_west_far():
        pl.when(to_up)(lambda: start(up_west))
        pl.when(to_down)(lambda: start(down_west))

    def start_west():
        pl.when(polar)(lambda: start(wide[1]))
        pl.when(jnp.logical_not(polar))(lambda: start(thin[1]))

    def start_lat():
        pl.when(has_up)(lambda: start(up))
        pl.when(has_down)(lambda: start(down))

    @pl.when(final)
    def _():
        tell_one(from_west, (la, east))
        start_east()
        tell_far(from_far, east)
        tell(barrier, west)

    pl.when(even & jnp.logical_not(final))(lambda: tell_lat(from_lat))

    @pl.when(inside)
    def _():
        tell(from_east, west)

        @pl.when(pivot)
        def _():
            tell_one(from_west, (la, east))
            tell_far(from_far, east)

    pl.when(even & jnp.logical_not(final))(start_lat)
    pl.when(inside)(start_west_far)
    pl.when(inside)(start_west)
    pl.when(pivot)(start_east)
    pl.when(jnp.logical_not(first))(fetch)

    prepare()
    body.wait()

    @pl.when(odd & jnp.logical_not(final))
    def _():
        pl.semaphore_wait(from_lat, beside)
        start_lat()

    @pl.when(rising)
    def _():
        pl.semaphore_wait(from_east, neighbours)
        start_east()

    @pl.when(final)
    def _():
        pl.semaphore_wait(from_west, 1)
        start_lat()
        pl.semaphore_wait(from_far, beside)
        start_west_far()
        start_west()

    def answer():
        pl.semaphore_wait(from_west, 1)
        start_west()

    def answer_far():
        pl.semaphore_wait(from_far, beside)
        start_west_far()

    def clear(row):
        S[:, row : row + 1, :] = jnp.zeros((S.shape[0], 1, CH), F32)

    pl.when(jnp.logical_not(has_down))(lambda: clear(7))
    pl.when(jnp.logical_not(has_up))(lambda: clear(40))

    pl.when(polar)(lambda: inner(1))
    pl.when(lo == 8)(answer)
    pl.when(polar)(lambda: inner(2))
    pl.when(lo == 0)(answer)
    pl.when(has_down)(lambda: wait_recv(up))
    pl.when(has_up)(lambda: wait_recv(down))

    @pl.when(polar)
    def _():
        inner(0)
        pl.when(lo == 8)(answer_far)
        inner(3)
        both_edges(True)
        pl.when(lo == 0)(answer_far)

        @pl.when(first)
        def _():
            close(True)
            close(False)

        @pl.when(jnp.logical_not(first))
        def _():
            close(False)
            close(True)

    @pl.when(jnp.logical_not(polar))
    def _():
        wait_recv(*thin)
        for t in range(TILES):
            plain(t)
        pl.when(first)(answer_far)

    pl.when(polar)(lambda: wait_send(*wide))
    pl.when(jnp.logical_not(polar))(lambda: wait_send(*thin))
    pl.when(has_up)(lambda: wait_send(up))
    pl.when(has_down)(lambda: wait_send(down))
    pl.when(to_up)(lambda: wait_send(up_east, up_west))
    pl.when(to_down)(lambda: wait_send(down_east, down_west))


def local(
    state, zonal_coef, diffusivity, coupling, filter_rows, band_width, table_index, coef_table
):
    turned = jnp.transpose(state, (1, 0, 2))
    args = (
        turned, zonal_coef[None, :], diffusivity[None, :], coupling,
        filter_rows[None, :], band_width[None, :], table_index[None, :], coef_table,
    )
    updated = pl.pallas_call(
        kernel,
        out_shape=pltpu.VMEM((COLS, ROWS, CH), F32),
        in_specs=[pl.BlockSpec(memory_space=pl.ANY)] * len(args),
        out_specs=pl.BlockSpec(memory_space=pltpu.VMEM),
        scratch_shapes=[
            pltpu.VMEM((COLS + 2 * HALO, ROWS + 16, CH), F32),
            pltpu.VMEM((TILES, COLS + 2 * MAXB, 8, CH), F32),
            pltpu.VMEM((MAXB + 1, TILES, 8, CH), F32),
            pltpu.VMEM((ROWS, CH), F32),
            pltpu.VMEM((ROWS, CH), F32),
            pltpu.VMEM((2 * CH, 2 * CH), BF16),
        ]
        + [pltpu.VMEM(a.shape, a.dtype) for a in args[1:]]
        + [
            pltpu.SemaphoreType.DMA((14,)),
            pltpu.SemaphoreType.DMA((14,)),
            pltpu.SemaphoreType.DMA((8,)),
            pltpu.SemaphoreType.REGULAR,
            pltpu.SemaphoreType.REGULAR,
            pltpu.SemaphoreType.REGULAR,
            pltpu.SemaphoreType.REGULAR,
        ],
        compiler_params=pltpu.CompilerParams(
            collective_id=0, has_side_effects=True, vmem_limit_bytes=56 * 1024 * 1024
        ),
    )(*args)
    return jnp.transpose(updated, (1, 0, 2))


def solution(mesh):
    return jax.shard_map(
        local,
        mesh=mesh,
        in_specs=(P("lat", "lon", None), P("lat"), P(), P(), P(), P(), P(), P()),
        out_specs=P("lat", "lon", None),
        check_vma=False,
    )
```

```python
import jax
import jax.numpy as jnp
from jax import lax
from jax.experimental import pallas as pl
from jax.experimental.pallas import tpu as pltpu
from jax.sharding import PartitionSpec as P

MAXB = 16
HALO = MAXB + 1
MERIDIONAL = 0.1
ROWS = 32
COLS = 225
CH = 128
TILES = ROWS // 8
CHUNK = COLS - 2
PLAIN = 75
BLOCK = 8
MESH = pl.DeviceIdType.MESH
F32 = jnp.float32
BF16 = jnp.bfloat16


def chunks(total, size):
    return [min(i * size, total - size) for i in range((total + size - 1) // size)]


def stepped(S, A, C0, df_v, t, q0, size):
    low = 8 + 8 * t
    centre = S[pl.ds(q0 + 1, size), low : low + 8, :]
    sides = S[pl.ds(q0 + 2, size), low : low + 8, :] + S[pl.ds(q0, size), low : low + 8, :]
    poles = (
        S[pl.ds(q0 + 1, size), low + 1 : low + 9, :] + S[pl.ds(q0 + 1, size), low - 1 : low + 7, :]
    )
    rows = slice(8 * t, 8 * t + 8)
    value = (
        C0[rows][None] * centre
        + A[rows][None] * sides
        + (MERIDIONAL * df_v[...])[None] * poles
    )
    return value.reshape(size * 8, CH)


def coupled(S, A, C0, R, df_v, *parts):
    flat = [stepped(S, A, C0, df_v, *part) for part in parts]
    flat = flat[0] if len(flat) == 1 else jnp.concatenate(flat, axis=0)
    big = flat.astype(BF16)
    small = (flat - big.astype(F32)).astype(BF16)
    wide = jnp.dot(jnp.concatenate([big, small], axis=1), R[...], preferred_element_type=F32)
    flat = flat + (wide[:, :CH] + wide[:, CH:])
    return flat.reshape(flat.shape[0] // 8, 8, CH)


def edge(C, W, source_of, target, t, right, known):
    place = [COLS - 1 - i if right else i for i in range(HALO)]
    rows = pl.ds(pl.multiple_of(8 * t, 8), 8)
    most = HALO + 2 * MAXB
    wanted = range(HALO, most) if known else range(HALO)
    source = {q: C[t, COLS + 2 * MAXB - 1 - q if right else q] for q in wanted}
    total = [None if known else source_of[i, rows, :] for i in place]
    for k in range(MAXB + 1):
        weight = W[k, t]
        for i in range(HALO):
            reached = sorted({i + MAXB - k, i + MAXB + k})
            values = [source[q] for q in reached if q in source]
            if values:
                value = weight * (values[0] if len(values) == 1 else values[0] + values[1])
                total[i] = value if total[i] is None else total[i] + value
    for i in range(HALO):
        target[place[i], rows, :] = total[i]


def finish(v, S, W, A, C0, R, df_v, out, C, E, sem):
    la = lax.axis_index("lat")
    open_edge = (lax.rem(lax.axis_index("lon"), 8) == 0) & ((la < 4) | (la >= 12))
    inner = pltpu.make_async_copy(v.at[HALO:COLS], out.at[HALO:COLS], sem.at[0])
    inner.start()

    @pl.when(open_edge)
    def _():
        value = coupled(S, A, C0, R, df_v, *[(t, 0, HALO) for t in range(TILES)])
        for t in range(TILES):
            C[t] = value[t * HALO : t * HALO + HALO]

        @pl.loop(0, TILES)
        def _(t):
            edge(C, W, v, E, t, False, False)

        rest = pltpu.make_async_copy(E, out.at[0:HALO], sem.at[1])
        rest.start()
        rest.wait()

    @pl.when(jnp.logical_not(open_edge))
    def _():
        rest = pltpu.make_async_copy(v.at[0:HALO], out.at[0:HALO], sem.at[1])
        rest.start()
        rest.wait()

    inner.wait()


def kernel(
    st, zc, df, cp, fr, bw, ti, ct, out, S, W, A, C0, R, df_v,
    C, zc_v, cp_v, fr_v, bw_v, ti_v, ct_v, ss, rs, ls,
    from_east, from_west, from_far, from_lat,
):
    la = lax.axis_index("lat")
    lo = lax.axis_index("lon")
    east = lax.rem(lo + 1, 16)
    west = lax.rem(lo + 15, 16)

    def is_polar(pos):
        return (pos < 4) | (pos >= 12)

    polar = is_polar(la)
    has_up = la < 15
    has_down = la > 0

    barrier = pltpu.get_barrier_semaphore()

    place = lax.rem(lo, 8)
    first = place == 0
    pivot = place == 6
    final = place == 7
    rising = place < 6
    inside = jnp.logical_not(first | final)
    beside = jnp.where(has_up, 1, 0) + jnp.where(has_down, 1, 0)
    neighbours = 1 + beside

    def tell_one(semaphore, device):
        pl.semaphore_signal(semaphore, inc=1, device_id=device, device_id_type=MESH)

    def tell_far(semaphore, side):
        pl.when(has_up)(lambda: tell_one(semaphore, (la + 1, side)))
        pl.when(has_down)(lambda: tell_one(semaphore, (la - 1, side)))

    def tell(semaphore, side):
        tell_one(semaphore, (la, side))
        tell_far(semaphore, side)

    def tell_lat(semaphore):
        tell_far(semaphore, lo)

    odd = lax.rem(la, 2) == 1
    even = jnp.logical_not(odd)
    pl.when(odd & jnp.logical_not(final))(lambda: tell_lat(barrier))
    pl.when(rising)(lambda: tell(barrier, east))
    pl.when(first)(lambda: tell(barrier, west))

    small = [(zc, zc_v), (df, df_v), (cp, cp_v), (fr, fr_v), (bw, bw_v), (ti, ti_v), (ct, ct_v)]
    loads = [pltpu.make_async_copy(src, dst, ls.at[i]) for i, (src, dst) in enumerate(small)]
    body = pltpu.make_async_copy(st, S.at[HALO : HALO + COLS, 8 : 8 + ROWS], ls.at[7])

    def fetch():
        for load in loads:
            load.start()
        body.start()

    pl.when(first)(fetch)

    def prepare():
        for load in loads:
            load.wait()

        def iota(shape, dim):
            return lax.broadcasted_iota(jnp.int32, shape, dim)

        def column(values, offset):
            width = values.shape[1]
            pick = iota((ROWS, width), 1) == iota((ROWS, width), 0) + offset
            return jnp.sum(jnp.where(pick, values.astype(F32), 0.0), axis=1, keepdims=True)

        zonal = column(zc_v[...], 0)
        spread = df_v[...]
        A[...] = zonal * spread
        C0[...] = 1.0 - 2.0 * (zonal + MERIDIONAL) * spread
        fine = cp_v[...]
        coarse = fine.astype(BF16)
        rest = (fine - coarse.astype(F32)).astype(BF16)
        both = jnp.concatenate([coarse, rest], axis=1)
        R[...] = jnp.concatenate([both, both], axis=0)

        @pl.when(polar)
        def _():
            first = la * ROWS
            tables = column(ti_v[...], first)
            widths = column(bw_v[...], first)
            same = fr_v[...] == iota((ROWS, fr_v.shape[1]), 0) + first
            listed = jnp.sum(jnp.where(same, 1.0, 0.0), axis=1, keepdims=True) > 0.5
            taps = ct_v.shape[1]
            picked = jnp.zeros((ROWS, taps), F32)
            for table in range(ct_v.shape[0]):
                picked = jnp.where(tables == float(table), ct_v[table : table + 1, :], picked)
            reach = iota((ROWS, taps), 1)
            picked = jnp.where(reach.astype(F32) <= widths, picked, 0.0)
            picked = jnp.where(listed, picked, jnp.where(reach == 0, 1.0, 0.0))
            for k in range(taps):
                W[k] = jnp.broadcast_to(picked[:, k : k + 1], (ROWS, CH)).reshape(TILES, 8, CH)

    def smooth(t, i0, size):
        window = [C[t, i0 + m] for m in range(size + 2 * MAXB)]
        total = [W[0, t] * window[b + MAXB] for b in range(size)]
        for k in range(1, MAXB + 1):
            weight = W[k, t]
            for b in range(size):
                total[b] = total[b] + weight * (window[b + MAXB - k] + window[b + MAXB + k])
        for b in range(size):
            out[i0 + b, pl.ds(pl.multiple_of(8 * t, 8), 8), :] = total[b]

    def inner(t):
        n = COLS - 2
        steps = (n + CHUNK - 1) // CHUNK

        @pl.loop(0, steps)
        def _(j):
            q0 = HALO + jnp.minimum(j * CHUNK, n - CHUNK)
            C[t, pl.ds(q0, CHUNK)] = coupled(S, A, C0, R, df_v, (t, q0, CHUNK))

        m = COLS - 2 * HALO
        steps = (m + BLOCK - 1) // BLOCK

        @pl.loop(0, steps)
        def _(j):
            smooth(t, HALO + jnp.minimum(j * BLOCK, m - BLOCK), BLOCK)

    def both_edges(known):
        @pl.loop(0, TILES)
        def _(t):
            edge(C, W, out, out, t, False, known)
            edge(C, W, out, out, t, True, known)

    def arrive(right):
        pl.when(has_down)(lambda: wait_recv(up_west if right else up_east))
        pl.when(has_up)(lambda: wait_recv(down_west if right else down_east))
        wait_recv(wide[1] if right else wide[0])

    def close(right):
        arrive(right)
        q0 = COLS + MAXB - 1 if right else 0
        value = coupled(S, A, C0, R, df_v, *[(t, q0, HALO) for t in range(TILES)])
        for t in range(TILES):
            C[t, q0 : q0 + HALO] = value[t * HALO : t * HALO + HALO]

        @pl.loop(0, TILES)
        def _(t):
            edge(C, W, out, out, t, right, False)

    def plain(t):
        @pl.loop(0, COLS // PLAIN)
        def _(j):
            i0 = j * PLAIN
            out[pl.ds(i0, PLAIN), 8 * t : 8 * t + 8, :] = coupled(S, A, C0, R, df_v, (t, i0 + MAXB, PLAIN))

    count = (
        jnp.where(odd | final, 0, beside)
        + jnp.where(inside, neighbours, 0)
        + jnp.where(pivot | final, neighbours, 0)
    )
    pl.when(count > 0)(lambda: pl.semaphore_wait(barrier, count))

    def send(src, dst, i, device):
        return pltpu.make_async_remote_copy(
            src_ref=src, dst_ref=dst, send_sem=ss.at[i], recv_sem=rs.at[i],
            device_id=device, device_id_type=MESH,
        )

    last = COLS - HALO
    high = HALO + COLS
    wide = (
        send(st.at[last:COLS], S.at[0:HALO, 8 : 8 + ROWS], 2, (la, east)),
        send(st.at[0:HALO], S.at[high : high + HALO, 8 : 8 + ROWS], 3, (la, west)),
    )
    thin = (
        send(st.at[COLS - 1 : COLS], S.at[HALO - 1 : HALO, 8 : 8 + ROWS], 0, (la, east)),
        send(st.at[0:1], S.at[high : high + 1, 8 : 8 + ROWS], 1, (la, west)),
    )
    up = send(st.at[:, 31:32], S.at[HALO:high, 7:8], 8, (la + 1, lo))
    down = send(st.at[:, 0:1], S.at[HALO:high, 40:41], 9, (la - 1, lo))
    up_east = send(st.at[last:COLS, 31:32], S.at[0:HALO, 7:8], 10, (la + 1, east))
    up_west = send(st.at[0:HALO, 31:32], S.at[high : high + HALO, 7:8], 11, (la + 1, west))
    down_east = send(st.at[last:COLS, 0:1], S.at[0:HALO, 40:41], 12, (la - 1, east))
    down_west = send(st.at[0:HALO, 0:1], S.at[high : high + HALO, 40:41], 13, (la - 1, west))

    def start(*copies):
        for copy in copies:
            copy.start()

    def wait_send(*copies):
        for copy in copies:
            copy.wait_send()

    def wait_recv(*copies):
        for copy in copies:
            copy.wait_recv()

    to_up = has_up & is_polar(la + 1)
    to_down = has_down & is_polar(la - 1)

    def start_east_far():
        pl.when(to_up)(lambda: start(up_east))
        pl.when(to_down)(lambda: start(down_east))

    def start_east():
        pl.when(polar)(lambda: start(wide[0]))
        pl.when(jnp.logical_not(polar))(lambda: start(thin[0]))

    def start_west_far():
        pl.when(to_up)(lambda: start(up_west))
        pl.when(to_down)(lambda: start(down_west))

    def start_west():
        pl.when(polar)(lambda: start(wide[1]))
        pl.when(jnp.logical_not(polar))(lambda: start(thin[1]))

    def start_lat():
        pl.when(has_up)(lambda: start(up))
        pl.when(has_down)(lambda: start(down))

    @pl.when(final)
    def _():
        tell_one(from_west, (la, east))
        start_east_far()
        late = (lo == 15) & ((la == 0) | (la == 3))
        pl.when(jnp.logical_not(late))(start_east)
        tell_far(from_far, east)
        tell(barrier, west)
        pl.when(late)(start_east)

    pl.when(even & jnp.logical_not(final))(lambda: tell_lat(from_lat))

    @pl.when(inside)
    def _():
        tell(from_east, west)

        @pl.when(pivot)
        def _():
            tell_one(from_west, (la, east))
            tell_far(from_far, east)

    pl.when(even & jnp.logical_not(final))(start_lat)
    pl.when(inside)(start_west_far)
    pl.when(inside)(start_west)
    pl.when(pivot)(start_east_far)
    pl.when(pivot)(start_east)
    pl.when(jnp.logical_not(first))(fetch)

    prepare()
    body.wait()

    pl.when(polar & first)(lambda: inner(1))

    @pl.when(odd & jnp.logical_not(final))
    def _():
        pl.semaphore_wait(from_lat, beside)
        start_lat()

    @pl.when(rising)
    def _():
        pl.semaphore_wait(from_east, neighbours)
        start_east_far()
        start_east()

    @pl.when(final)
    def _():
        pl.semaphore_wait(from_west, 1)
        start_lat()
        pl.semaphore_wait(from_far, beside)
        start_west_far()
        start_west()

    def answer():
        pl.semaphore_wait(from_west, 1)
        start_west()

    def answer_far():
        pl.semaphore_wait(from_far, beside)
        start_west_far()

    def clear(row):
        S[:, row : row + 1, :] = jnp.zeros((S.shape[0], 1, CH), F32)

    pl.when(jnp.logical_not(has_down))(lambda: clear(7))
    pl.when(jnp.logical_not(has_up))(lambda: clear(40))

    pl.when(polar & jnp.logical_not(first))(lambda: inner(1))
    pl.when(lo == 8)(answer)
    pl.when(polar)(lambda: inner(2))
    pl.when((lo == 0) & jnp.logical_not(polar))(answer)
    pl.when(has_down)(lambda: wait_recv(up))
    pl.when(has_up)(lambda: wait_recv(down))

    @pl.when(polar)
    def _():
        inner(0)
        pl.when(lo == 0)(answer)
        pl.when(lo == 8)(answer_far)
        inner(3)
        both_edges(True)

        @pl.when(first)
        def _():
            close(True)
            pl.when(lo == 0)(answer_far)
            arrive(False)

        @pl.when(jnp.logical_not(first))
        def _():
            close(False)
            close(True)

    @pl.when(jnp.logical_not(polar))
    def _():
        wait_recv(*thin)
        for t in range(TILES):
            plain(t)
        pl.when(first)(answer_far)

    pl.when(polar)(lambda: wait_send(*wide))
    pl.when(jnp.logical_not(polar))(lambda: wait_send(*thin))
    pl.when(has_up)(lambda: wait_send(up))
    pl.when(has_down)(lambda: wait_send(down))
    pl.when(to_up)(lambda: wait_send(up_east, up_west))
    pl.when(to_down)(lambda: wait_send(down_east, down_west))


def local(
    state, zonal_coef, diffusivity, coupling, filter_rows, band_width, table_index, coef_table
):
    turned = jnp.transpose(state, (1, 0, 2))
    args = (
        turned, zonal_coef[None, :], diffusivity[None, :], coupling,
        filter_rows[None, :], band_width[None, :], table_index[None, :], coef_table,
    )
    vmem = pl.BlockSpec(memory_space=pltpu.VMEM)
    parts = pl.pallas_call(
        kernel,
        out_shape=(
            pltpu.VMEM((COLS, ROWS, CH), F32),
            pltpu.VMEM((COLS + 2 * HALO, ROWS + 16, CH), F32),
            pltpu.VMEM((MAXB + 1, TILES, 8, CH), F32),
            pltpu.VMEM((ROWS, CH), F32),
            pltpu.VMEM((ROWS, CH), F32),
            pltpu.VMEM((2 * CH, 2 * CH), BF16),
            pltpu.VMEM((1, CH), F32),
        ),
        in_specs=[pl.BlockSpec(memory_space=pltpu.HBM)] * len(args),
        out_specs=(vmem,) * 7,
        scratch_shapes=[pltpu.VMEM((TILES, COLS + 2 * MAXB, 8, CH), F32)]
        + [pltpu.VMEM(args[i].shape, args[i].dtype) for i in (1, 3, 4, 5, 6, 7)]
        + [
            pltpu.SemaphoreType.DMA((14,)),
            pltpu.SemaphoreType.DMA((14,)),
            pltpu.SemaphoreType.DMA((8,)),
            pltpu.SemaphoreType.REGULAR,
            pltpu.SemaphoreType.REGULAR,
            pltpu.SemaphoreType.REGULAR,
            pltpu.SemaphoreType.REGULAR,
        ],
        compiler_params=pltpu.CompilerParams(
            collective_id=0, has_side_effects=True, vmem_limit_bytes=53 * 1024 * 1024
        ),
    )(*args)
    updated = pl.pallas_call(
        finish,
        out_shape=pltpu.HBM((COLS, ROWS, CH), F32),
        in_specs=[vmem] * 7,
        out_specs=pl.BlockSpec(memory_space=pltpu.HBM),
        scratch_shapes=[
            pltpu.VMEM((TILES, HALO, 8, CH), F32),
            pltpu.VMEM((HALO, ROWS, CH), F32),
            pltpu.SemaphoreType.DMA((2,)),
        ],
        compiler_params=pltpu.CompilerParams(vmem_limit_bytes=32 * 1024 * 1024),
    )(*parts)
    return jnp.transpose(updated, (1, 0, 2))


def solution(mesh):
    return jax.shard_map(
        local,
        mesh=mesh,
        in_specs=(P("lat", "lon", None), P("lat"), P(), P(), P(), P(), P(), P()),
        out_specs=P("lat", "lon", None),
        check_vma=False,
    )
```

```python
import jax
import jax.numpy as jnp
from jax import lax
from jax.experimental import pallas as pl
from jax.experimental.pallas import tpu as pltpu
from jax.sharding import PartitionSpec as P

MAXB = 16
HALO = MAXB + 1
MERIDIONAL = 0.1
ROWS = 32
COLS = 225
CH = 128
TILES = ROWS // 8
CHUNK = COLS - 2
PLAIN = 75
BLOCK = 8
MESH = pl.DeviceIdType.MESH
F32 = jnp.float32
BF16 = jnp.bfloat16


def chunks(total, size):
    return [min(i * size, total - size) for i in range((total + size - 1) // size)]


def stepped(S, A, C0, df_v, t, q0, size):
    low = 8 + 8 * t
    centre = S[pl.ds(q0 + 1, size), low : low + 8, :]
    sides = S[pl.ds(q0 + 2, size), low : low + 8, :] + S[pl.ds(q0, size), low : low + 8, :]
    poles = (
        S[pl.ds(q0 + 1, size), low + 1 : low + 9, :] + S[pl.ds(q0 + 1, size), low - 1 : low + 7, :]
    )
    rows = slice(8 * t, 8 * t + 8)
    value = (
        C0[rows][None] * centre
        + A[rows][None] * sides
        + (MERIDIONAL * df_v[...])[None] * poles
    )
    return value.reshape(size * 8, CH)


def coupled(S, A, C0, R, df_v, *parts):
    flat = [stepped(S, A, C0, df_v, *part) for part in parts]
    flat = flat[0] if len(flat) == 1 else jnp.concatenate(flat, axis=0)
    big = flat.astype(BF16)
    small = (flat - big.astype(F32)).astype(BF16)
    wide = jnp.dot(jnp.concatenate([big, small], axis=1), R[...], preferred_element_type=F32)
    flat = flat + (wide[:, :CH] + wide[:, CH:])
    return flat.reshape(flat.shape[0] // 8, 8, CH)


class Moved:
    def __init__(self, ref, shift):
        self.ref, self.shift = ref, shift

    def at(self, index):
        if self.ref.ndim == 4:
            return (index[0], index[1] + self.shift)
        return (index[0] + self.shift,) + index[1:]

    def __getitem__(self, index):
        return self.ref[self.at(index)]

    def __setitem__(self, index, value):
        self.ref[self.at(index)] = value


def edge(C, W, source_of, target, t, right, known):
    place = [COLS - 1 - i if right else i for i in range(HALO)]
    rows = pl.ds(pl.multiple_of(8 * t, 8), 8)
    most = HALO + 2 * MAXB
    wanted = range(HALO, most) if known else range(HALO)
    source = {q: C[t, COLS + 2 * MAXB - 1 - q if right else q] for q in wanted}
    total = [None if known else source_of[i, rows, :] for i in place]
    for k in range(MAXB + 1):
        weight = W[k, t]
        for i in range(HALO):
            reached = sorted({i + MAXB - k, i + MAXB + k})
            values = [source[q] for q in reached if q in source]
            if values:
                value = weight * (values[0] if len(values) == 1 else values[0] + values[1])
                total[i] = value if total[i] is None else total[i] + value
    for i in range(HALO):
        target[place[i], rows, :] = total[i]


def finish(v, S, W, A, C0, R, df_v, out, C, E, sem):
    la = lax.axis_index("lat")
    polar = (la < 4) | (la >= 12)
    high = COLS - HALO
    inner = pltpu.make_async_copy(v.at[HALO:high], out.at[HALO:high], sem.at[0])
    inner.start()

    def write(low, high):
        left = pltpu.make_async_copy(low, out.at[0:HALO], sem.at[1])
        right = pltpu.make_async_copy(high, out.at[COLS - HALO : COLS], sem.at[2])
        left.start()
        right.start()
        left.wait()
        right.wait()

    @pl.when(polar)
    def _():
        far = COLS + MAXB - 1
        parts = [(t, q0, HALO) for t in range(TILES) for q0 in (0, far)]
        value = coupled(S, A, C0, R, df_v, *parts)
        for i, (t, q0, size) in enumerate(parts):
            C[t, (i % 2) * size : (i % 2) * size + size] = value[i * size : i * size + size]

        @pl.loop(0, TILES)
        def _(t):
            edge(Moved(C, 0), W, v, Moved(E, 0), t, False, False)
            edge(Moved(C, HALO - far), W, v, Moved(E, HALO - high), t, True, False)

        write(E.at[0:HALO], E.at[HALO : 2 * HALO])

    @pl.when(jnp.logical_not(polar))
    def _():
        write(v.at[0:HALO], v.at[high:COLS])

    inner.wait()


def kernel(
    st, zc, df, cp, fr, bw, ti, ct, out, S, W, A, C0, R, df_v,
    C, zc_v, cp_v, fr_v, bw_v, ti_v, ct_v, ss, rs, ls,
    from_east, from_west, from_far, from_lat,
):
    la = lax.axis_index("lat")
    lo = lax.axis_index("lon")
    east = lax.rem(lo + 1, 16)
    west = lax.rem(lo + 15, 16)

    def is_polar(pos):
        return (pos < 4) | (pos >= 12)

    polar = is_polar(la)
    has_up = la < 15
    has_down = la > 0

    barrier = pltpu.get_barrier_semaphore()

    place = lax.rem(lo, 8)
    first = place == 0
    pivot = place == 6
    final = place == 7
    rising = place < 6
    inside = jnp.logical_not(first | final)
    beside = jnp.where(has_up, 1, 0) + jnp.where(has_down, 1, 0)
    neighbours = 1 + beside

    def tell_one(semaphore, device):
        pl.semaphore_signal(semaphore, inc=1, device_id=device, device_id_type=MESH)

    def tell_far(semaphore, side):
        pl.when(has_up)(lambda: tell_one(semaphore, (la + 1, side)))
        pl.when(has_down)(lambda: tell_one(semaphore, (la - 1, side)))

    def tell(semaphore, side):
        tell_one(semaphore, (la, side))
        tell_far(semaphore, side)

    def tell_lat(semaphore):
        tell_far(semaphore, lo)

    odd = lax.rem(la, 2) == 1
    even = jnp.logical_not(odd)
    pl.when(odd & jnp.logical_not(final))(lambda: tell_lat(barrier))
    pl.when(rising)(lambda: tell(barrier, east))
    pl.when(first)(lambda: tell(barrier, west))

    small = [(zc, zc_v), (df, df_v), (cp, cp_v), (fr, fr_v), (bw, bw_v), (ti, ti_v), (ct, ct_v)]
    loads = [pltpu.make_async_copy(src, dst, ls.at[i]) for i, (src, dst) in enumerate(small)]
    body = pltpu.make_async_copy(st, S.at[HALO : HALO + COLS, 8 : 8 + ROWS], ls.at[7])

    def fetch():
        for load in loads:
            load.start()
        body.start()

    pl.when(first)(fetch)

    def prepare():
        for load in loads:
            load.wait()

        def iota(shape, dim):
            return lax.broadcasted_iota(jnp.int32, shape, dim)

        def column(values, offset):
            width = values.shape[1]
            pick = iota((ROWS, width), 1) == iota((ROWS, width), 0) + offset
            return jnp.sum(jnp.where(pick, values.astype(F32), 0.0), axis=1, keepdims=True)

        zonal = column(zc_v[...], 0)
        spread = df_v[...]
        A[...] = zonal * spread
        C0[...] = 1.0 - 2.0 * (zonal + MERIDIONAL) * spread
        fine = cp_v[...]
        coarse = fine.astype(BF16)
        rest = (fine - coarse.astype(F32)).astype(BF16)
        both = jnp.concatenate([coarse, rest], axis=1)
        R[...] = jnp.concatenate([both, both], axis=0)

        @pl.when(polar)
        def _():
            first = la * ROWS
            tables = column(ti_v[...], first)
            widths = column(bw_v[...], first)
            same = fr_v[...] == iota((ROWS, fr_v.shape[1]), 0) + first
            listed = jnp.sum(jnp.where(same, 1.0, 0.0), axis=1, keepdims=True) > 0.5
            taps = ct_v.shape[1]
            picked = jnp.zeros((ROWS, taps), F32)
            for table in range(ct_v.shape[0]):
                picked = jnp.where(tables == float(table), ct_v[table : table + 1, :], picked)
            reach = iota((ROWS, taps), 1)
            picked = jnp.where(reach.astype(F32) <= widths, picked, 0.0)
            picked = jnp.where(listed, picked, jnp.where(reach == 0, 1.0, 0.0))
            for k in range(taps):
                W[k] = jnp.broadcast_to(picked[:, k : k + 1], (ROWS, CH)).reshape(TILES, 8, CH)

    def smooth(t, i0, size):
        window = [C[t, i0 + m] for m in range(size + 2 * MAXB)]
        total = [W[0, t] * window[b + MAXB] for b in range(size)]
        for k in range(1, MAXB + 1):
            weight = W[k, t]
            for b in range(size):
                total[b] = total[b] + weight * (window[b + MAXB - k] + window[b + MAXB + k])
        for b in range(size):
            out[i0 + b, pl.ds(pl.multiple_of(8 * t, 8), 8), :] = total[b]

    def inner(t):
        n = COLS - 2
        steps = (n + CHUNK - 1) // CHUNK

        @pl.loop(0, steps)
        def _(j):
            q0 = HALO + jnp.minimum(j * CHUNK, n - CHUNK)
            C[t, pl.ds(q0, CHUNK)] = coupled(S, A, C0, R, df_v, (t, q0, CHUNK))

        m = COLS - 2 * HALO
        steps = (m + BLOCK - 1) // BLOCK

        @pl.loop(0, steps)
        def _(j):
            smooth(t, HALO + jnp.minimum(j * BLOCK, m - BLOCK), BLOCK)

    def both_edges(known):
        @pl.loop(0, TILES)
        def _(t):
            edge(C, W, out, out, t, False, known)
            edge(C, W, out, out, t, True, known)

    def arrive(right):
        pl.when(has_down)(lambda: wait_recv(up_west if right else up_east))
        pl.when(has_up)(lambda: wait_recv(down_west if right else down_east))
        wait_recv(wide[1] if right else wide[0])

    def plain(t):
        @pl.loop(0, COLS // PLAIN)
        def _(j):
            i0 = j * PLAIN
            out[pl.ds(i0, PLAIN), 8 * t : 8 * t + 8, :] = coupled(S, A, C0, R, df_v, (t, i0 + MAXB, PLAIN))

    count = (
        jnp.where(odd | final, 0, beside)
        + jnp.where(inside, neighbours, 0)
        + jnp.where(pivot | final, neighbours, 0)
    )
    pl.when(count > 0)(lambda: pl.semaphore_wait(barrier, count))

    def send(src, dst, i, device):
        return pltpu.make_async_remote_copy(
            src_ref=src, dst_ref=dst, send_sem=ss.at[i], recv_sem=rs.at[i],
            device_id=device, device_id_type=MESH,
        )

    last = COLS - HALO
    high = HALO + COLS
    wide = (
        send(st.at[last:COLS], S.at[0:HALO, 8 : 8 + ROWS], 2, (la, east)),
        send(st.at[0:HALO], S.at[high : high + HALO, 8 : 8 + ROWS], 3, (la, west)),
    )
    thin = (
        send(st.at[COLS - 1 : COLS], S.at[HALO - 1 : HALO, 8 : 8 + ROWS], 0, (la, east)),
        send(st.at[0:1], S.at[high : high + 1, 8 : 8 + ROWS], 1, (la, west)),
    )
    up = send(st.at[:, 31:32], S.at[HALO:high, 7:8], 8, (la + 1, lo))
    down = send(st.at[:, 0:1], S.at[HALO:high, 40:41], 9, (la - 1, lo))
    up_east = send(st.at[last:COLS, 31:32], S.at[0:HALO, 7:8], 10, (la + 1, east))
    up_west = send(st.at[0:HALO, 31:32], S.at[high : high + HALO, 7:8], 11, (la + 1, west))
    down_east = send(st.at[last:COLS, 0:1], S.at[0:HALO, 40:41], 12, (la - 1, east))
    down_west = send(st.at[0:HALO, 0:1], S.at[high : high + HALO, 40:41], 13, (la - 1, west))

    def start(*copies):
        for copy in copies:
            copy.start()

    def wait_send(*copies):
        for copy in copies:
            copy.wait_send()

    def wait_recv(*copies):
        for copy in copies:
            copy.wait_recv()

    to_up = has_up & is_polar(la + 1)
    to_down = has_down & is_polar(la - 1)

    def start_east_far():
        pl.when(to_up)(lambda: start(up_east))
        pl.when(to_down)(lambda: start(down_east))

    def start_east():
        pl.when(polar)(lambda: start(wide[0]))
        pl.when(jnp.logical_not(polar))(lambda: start(thin[0]))

    def start_west_far():
        pl.when(to_up)(lambda: start(up_west))
        pl.when(to_down)(lambda: start(down_west))

    def start_west():
        pl.when(polar)(lambda: start(wide[1]))
        pl.when(jnp.logical_not(polar))(lambda: start(thin[1]))

    def start_lat():
        pl.when(has_up)(lambda: start(up))
        pl.when(has_down)(lambda: start(down))

    @pl.when(final)
    def _():
        tell_one(from_west, (la, east))
        start_east_far()
        late = (lo == 15) & ((la == 0) | (la == 3))
        pl.when(jnp.logical_not(late))(start_east)
        tell_far(from_far, east)
        tell(barrier, west)
        pl.when(late)(start_east)

    pl.when(even & jnp.logical_not(final))(lambda: tell_lat(from_lat))

    @pl.when(inside)
    def _():
        tell(from_east, west)

        @pl.when(pivot)
        def _():
            tell_one(from_west, (la, east))
            tell_far(from_far, east)

    pl.when(even & jnp.logical_not(final))(start_lat)
    pl.when(inside)(start_west_far)
    pl.when(inside)(start_west)
    pl.when(pivot)(start_east_far)
    pl.when(pivot)(start_east)
    pl.when(jnp.logical_not(first))(fetch)

    prepare()
    body.wait()

    pl.when(polar & first)(lambda: inner(1))

    @pl.when(odd & jnp.logical_not(final))
    def _():
        pl.semaphore_wait(from_lat, beside)
        start_lat()

    @pl.when(rising)
    def _():
        pl.semaphore_wait(from_east, neighbours)
        start_east_far()
        start_east()

    @pl.when(final)
    def _():
        pl.semaphore_wait(from_west, 1)
        start_lat()
        pl.semaphore_wait(from_far, beside)
        start_west_far()
        start_west()

    def answer():
        pl.semaphore_wait(from_west, 1)
        start_west()

    def answer_far():
        pl.semaphore_wait(from_far, beside)
        start_west_far()

    def clear(row):
        S[:, row : row + 1, :] = jnp.zeros((S.shape[0], 1, CH), F32)

    pl.when(jnp.logical_not(has_down))(lambda: clear(7))
    pl.when(jnp.logical_not(has_up))(lambda: clear(40))

    pl.when(polar & jnp.logical_not(first))(lambda: inner(1))
    pl.when(lo == 8)(answer)
    pl.when(polar)(lambda: inner(2))
    pl.when((lo == 0) & jnp.logical_not(polar))(answer)
    pl.when(has_down)(lambda: wait_recv(up))
    pl.when(has_up)(lambda: wait_recv(down))

    @pl.when(polar)
    def _():
        inner(0)
        pl.when(lo == 0)(answer)
        pl.when(lo == 8)(answer_far)
        inner(3)
        both_edges(True)

        arrive(True)
        pl.when(lo == 0)(answer_far)
        arrive(False)

    @pl.when(jnp.logical_not(polar))
    def _():
        wait_recv(*thin)
        for t in range(TILES):
            plain(t)
        pl.when(first)(answer_far)

    pl.when(polar)(lambda: wait_send(*wide))
    pl.when(jnp.logical_not(polar))(lambda: wait_send(*thin))
    pl.when(has_up)(lambda: wait_send(up))
    pl.when(has_down)(lambda: wait_send(down))
    pl.when(to_up)(lambda: wait_send(up_east, up_west))
    pl.when(to_down)(lambda: wait_send(down_east, down_west))


def local(
    state, zonal_coef, diffusivity, coupling, filter_rows, band_width, table_index, coef_table
):
    turned = jnp.transpose(state, (1, 0, 2))
    args = (
        turned, zonal_coef[None, :], diffusivity[None, :], coupling,
        filter_rows[None, :], band_width[None, :], table_index[None, :], coef_table,
    )
    vmem = pl.BlockSpec(memory_space=pltpu.VMEM)
    parts = pl.pallas_call(
        kernel,
        out_shape=(
            pltpu.VMEM((COLS, ROWS, CH), F32),
            pltpu.VMEM((COLS + 2 * HALO, ROWS + 16, CH), F32),
            pltpu.VMEM((MAXB + 1, TILES, 8, CH), F32),
            pltpu.VMEM((ROWS, CH), F32),
            pltpu.VMEM((ROWS, CH), F32),
            pltpu.VMEM((2 * CH, 2 * CH), BF16),
            pltpu.VMEM((1, CH), F32),
        ),
        in_specs=[pl.BlockSpec(memory_space=pltpu.HBM)] * len(args),
        out_specs=(vmem,) * 7,
        scratch_shapes=[pltpu.VMEM((TILES, COLS + 2 * MAXB, 8, CH), F32)]
        + [pltpu.VMEM(args[i].shape, args[i].dtype) for i in (1, 3, 4, 5, 6, 7)]
        + [
            pltpu.SemaphoreType.DMA((14,)),
            pltpu.SemaphoreType.DMA((14,)),
            pltpu.SemaphoreType.DMA((8,)),
            pltpu.SemaphoreType.REGULAR,
            pltpu.SemaphoreType.REGULAR,
            pltpu.SemaphoreType.REGULAR,
            pltpu.SemaphoreType.REGULAR,
        ],
        compiler_params=pltpu.CompilerParams(
            collective_id=0, has_side_effects=True, vmem_limit_bytes=53 * 1024 * 1024
        ),
    )(*args)
    updated = pl.pallas_call(
        finish,
        out_shape=pltpu.HBM((COLS, ROWS, CH), F32),
        in_specs=[vmem] * 7,
        out_specs=pl.BlockSpec(memory_space=pltpu.HBM),
        scratch_shapes=[
            pltpu.VMEM((TILES, 2 * HALO, 8, CH), F32),
            pltpu.VMEM((2 * HALO, ROWS, CH), F32),
            pltpu.SemaphoreType.DMA((3,)),
        ],
        compiler_params=pltpu.CompilerParams(vmem_limit_bytes=32 * 1024 * 1024),
    )(*parts)
    return jnp.transpose(updated, (1, 0, 2))


def solution(mesh):
    return jax.shard_map(
        local,
        mesh=mesh,
        in_specs=(P("lat", "lon", None), P("lat"), P(), P(), P(), P(), P(), P()),
        out_specs=P("lat", "lon", None),
        check_vma=False,
    )
```

```python
import jax
import jax.numpy as jnp
from jax import lax
from jax.experimental import pallas as pl
from jax.experimental.pallas import tpu as pltpu
from jax.sharding import PartitionSpec as P

MAXB = 16
HALO = MAXB + 1
MERIDIONAL = 0.1
ROWS = 32
COLS = 225
CH = 128
TILES = ROWS // 8
CHUNK = COLS - 2
PLAIN = 75
BLOCK = 8
MESH = pl.DeviceIdType.MESH
F32 = jnp.float32
BF16 = jnp.bfloat16


def chunks(total, size):
    return [min(i * size, total - size) for i in range((total + size - 1) // size)]


def stepped(S, A, C0, df_v, t, q0, size):
    low = 8 + 8 * t
    centre = S[pl.ds(q0 + 1, size), low : low + 8, :]
    sides = S[pl.ds(q0 + 2, size), low : low + 8, :] + S[pl.ds(q0, size), low : low + 8, :]
    poles = (
        S[pl.ds(q0 + 1, size), low + 1 : low + 9, :] + S[pl.ds(q0 + 1, size), low - 1 : low + 7, :]
    )
    rows = slice(8 * t, 8 * t + 8)
    value = (
        C0[rows][None] * centre
        + A[rows][None] * sides
        + (MERIDIONAL * df_v[...])[None] * poles
    )
    return value.reshape(size * 8, CH)


def coupled(S, A, C0, R, df_v, *parts):
    flat = [stepped(S, A, C0, df_v, *part) for part in parts]
    flat = flat[0] if len(flat) == 1 else jnp.concatenate(flat, axis=0)
    big = flat.astype(BF16)
    small = (flat - big.astype(F32)).astype(BF16)
    wide = jnp.dot(jnp.concatenate([big, small], axis=1), R[...], preferred_element_type=F32)
    flat = flat + (wide[:, :CH] + wide[:, CH:])
    return flat.reshape(flat.shape[0] // 8, 8, CH)


class Moved:
    def __init__(self, ref, shift):
        self.ref, self.shift = ref, shift

    def at(self, index):
        if self.ref.ndim == 4:
            return (index[0], index[1] + self.shift)
        return (index[0] + self.shift,) + index[1:]

    def __getitem__(self, index):
        return self.ref[self.at(index)]

    def __setitem__(self, index, value):
        self.ref[self.at(index)] = value


def edge(C, W, source_of, target, t, right, known):
    place = [COLS - 1 - i if right else i for i in range(HALO)]
    rows = pl.ds(pl.multiple_of(8 * t, 8), 8)
    most = HALO + 2 * MAXB
    wanted = range(HALO, most) if known else range(HALO)
    source = {q: C[t, COLS + 2 * MAXB - 1 - q if right else q] for q in wanted}
    total = [None if known else source_of[i, rows, :] for i in place]
    for k in range(MAXB + 1):
        weight = W[k, t]
        for i in range(HALO):
            reached = sorted({i + MAXB - k, i + MAXB + k})
            values = [source[q] for q in reached if q in source]
            if values:
                value = weight * (values[0] if len(values) == 1 else values[0] + values[1])
                total[i] = value if total[i] is None else total[i] + value
    for i in range(HALO):
        target[place[i], rows, :] = total[i]


def finish(v, S, W, A, C0, R, df_v, out, C, E, sem):
    la = lax.axis_index("lat")
    polar = (la < 4) | (la >= 12)
    high = COLS - HALO
    inner = pltpu.make_async_copy(v.at[HALO:high], out.at[HALO:high], sem.at[0])
    inner.start()

    def write(low, high):
        left = pltpu.make_async_copy(low, out.at[0:HALO], sem.at[1])
        right = pltpu.make_async_copy(high, out.at[COLS - HALO : COLS], sem.at[2])
        left.start()
        right.start()
        left.wait()
        right.wait()

    @pl.when(polar)
    def _():
        far = COLS + MAXB - 1
        parts = [(t, q0, HALO) for t in range(TILES) for q0 in (0, far)]
        value = coupled(S, A, C0, R, df_v, *parts)
        for i, (t, q0, size) in enumerate(parts):
            C[t, (i % 2) * size : (i % 2) * size + size] = value[i * size : i * size + size]

        @pl.loop(0, TILES)
        def _(t):
            edge(Moved(C, 0), W, v, Moved(E, 0), t, False, False)
            edge(Moved(C, HALO - far), W, v, Moved(E, HALO - high), t, True, False)

        write(E.at[0:HALO], E.at[HALO : 2 * HALO])

    @pl.when(jnp.logical_not(polar))
    def _():
        write(v.at[0:HALO], v.at[high:COLS])

    inner.wait()


def kernel(
    st, zc, df, cp, fr, bw, ti, ct, out, S, W, A, C0, R, df_v,
    C, zc_v, cp_v, fr_v, bw_v, ti_v, ct_v, ss, rs, ls,
    from_east, from_west, from_far, from_lat,
):
    la = lax.axis_index("lat")
    lo = lax.axis_index("lon")
    east = lax.rem(lo + 1, 16)
    west = lax.rem(lo + 15, 16)

    def is_polar(pos):
        return (pos < 4) | (pos >= 12)

    polar = is_polar(la)
    has_up = la < 15
    has_down = la > 0

    barrier = pltpu.get_barrier_semaphore()

    place = lax.rem(lo, 8)
    first = place == 0
    pivot = place == 6
    final = place == 7
    rising = place < 6
    inside = jnp.logical_not(first | final)
    beside = jnp.where(has_up, 1, 0) + jnp.where(has_down, 1, 0)
    neighbours = 1 + beside

    def tell_one(semaphore, device):
        pl.semaphore_signal(semaphore, inc=1, device_id=device, device_id_type=MESH)

    def tell_far(semaphore, side):
        pl.when(has_up)(lambda: tell_one(semaphore, (la + 1, side)))
        pl.when(has_down)(lambda: tell_one(semaphore, (la - 1, side)))

    def tell(semaphore, side):
        tell_one(semaphore, (la, side))
        tell_far(semaphore, side)

    def tell_lat(semaphore):
        tell_far(semaphore, lo)

    odd = lax.rem(la, 2) == 1
    even = jnp.logical_not(odd)
    pl.when(odd & jnp.logical_not(final))(lambda: tell_lat(barrier))
    pl.when(rising)(lambda: tell(barrier, east))
    pl.when(first)(lambda: tell(barrier, west))

    small = [(zc, zc_v), (df, df_v), (cp, cp_v), (fr, fr_v), (bw, bw_v), (ti, ti_v), (ct, ct_v)]
    loads = [pltpu.make_async_copy(src, dst, ls.at[i]) for i, (src, dst) in enumerate(small)]
    body = pltpu.make_async_copy(st, S.at[HALO : HALO + COLS, 8 : 8 + ROWS], ls.at[7])

    def fetch():
        for load in loads:
            load.start()
        body.start()

    pl.when(first)(fetch)

    def prepare():
        for load in loads:
            load.wait()

        def iota(shape, dim):
            return lax.broadcasted_iota(jnp.int32, shape, dim)

        def column(values, offset):
            width = values.shape[1]
            pick = iota((ROWS, width), 1) == iota((ROWS, width), 0) + offset
            return jnp.sum(jnp.where(pick, values.astype(F32), 0.0), axis=1, keepdims=True)

        zonal = column(zc_v[...], 0)
        spread = df_v[...]
        A[...] = zonal * spread
        C0[...] = 1.0 - 2.0 * (zonal + MERIDIONAL) * spread
        fine = cp_v[...]
        coarse = fine.astype(BF16)
        rest = (fine - coarse.astype(F32)).astype(BF16)
        both = jnp.concatenate([coarse, rest], axis=1)
        R[...] = jnp.concatenate([both, both], axis=0)

        @pl.when(polar)
        def _():
            first = la * ROWS
            tables = column(ti_v[...], first)
            widths = column(bw_v[...], first)
            same = fr_v[...] == iota((ROWS, fr_v.shape[1]), 0) + first
            listed = jnp.sum(jnp.where(same, 1.0, 0.0), axis=1, keepdims=True) > 0.5
            taps = ct_v.shape[1]
            picked = jnp.zeros((ROWS, taps), F32)
            for table in range(ct_v.shape[0]):
                picked = jnp.where(tables == float(table), ct_v[table : table + 1, :], picked)
            reach = iota((ROWS, taps), 1)
            picked = jnp.where(reach.astype(F32) <= widths, picked, 0.0)
            picked = jnp.where(listed, picked, jnp.where(reach == 0, 1.0, 0.0))
            for k in range(taps):
                W[k] = jnp.broadcast_to(picked[:, k : k + 1], (ROWS, CH)).reshape(TILES, 8, CH)

    def smooth(t, i0, size):
        window = [C[t, i0 + m] for m in range(size + 2 * MAXB)]
        total = [W[0, t] * window[b + MAXB] for b in range(size)]
        for k in range(1, MAXB + 1):
            weight = W[k, t]
            for b in range(size):
                total[b] = total[b] + weight * (window[b + MAXB - k] + window[b + MAXB + k])
        for b in range(size):
            out[i0 + b, pl.ds(pl.multiple_of(8 * t, 8), 8), :] = total[b]

    def inner(t):
        n = COLS - 2
        steps = (n + CHUNK - 1) // CHUNK

        @pl.loop(0, steps)
        def _(j):
            q0 = HALO + jnp.minimum(j * CHUNK, n - CHUNK)
            C[t, pl.ds(q0, CHUNK)] = coupled(S, A, C0, R, df_v, (t, q0, CHUNK))

        m = COLS - 2 * HALO
        steps = (m + BLOCK - 1) // BLOCK

        @pl.loop(0, steps)
        def _(j):
            smooth(t, HALO + jnp.minimum(j * BLOCK, m - BLOCK), BLOCK)

    def both_edges(known):
        @pl.loop(0, TILES)
        def _(t):
            edge(C, W, out, out, t, False, known)
            edge(C, W, out, out, t, True, known)

    def arrive(right):
        pl.when(has_down)(lambda: wait_recv(up_west if right else up_east))
        pl.when(has_up)(lambda: wait_recv(down_west if right else down_east))
        wait_recv(wide[1] if right else wide[0])

    def plain(t):
        @pl.loop(0, COLS // PLAIN)
        def _(j):
            i0 = j * PLAIN
            out[pl.ds(i0, PLAIN), 8 * t : 8 * t + 8, :] = coupled(S, A, C0, R, df_v, (t, i0 + MAXB, PLAIN))

    count = (
        jnp.where(odd | final, 0, beside)
        + jnp.where(inside, neighbours, 0)
        + jnp.where(pivot | final, neighbours, 0)
    )
    pl.when(count > 0)(lambda: pl.semaphore_wait(barrier, count))

    def send(src, dst, i, device):
        return pltpu.make_async_remote_copy(
            src_ref=src, dst_ref=dst, send_sem=ss.at[i], recv_sem=rs.at[i],
            device_id=device, device_id_type=MESH,
        )

    last = COLS - HALO
    high = HALO + COLS
    wide = (
        send(st.at[last:COLS], S.at[0:HALO, 8 : 8 + ROWS], 2, (la, east)),
        send(st.at[0:HALO], S.at[high : high + HALO, 8 : 8 + ROWS], 3, (la, west)),
    )
    thin = (
        send(st.at[COLS - 1 : COLS], S.at[HALO - 1 : HALO, 8 : 8 + ROWS], 0, (la, east)),
        send(st.at[0:1], S.at[high : high + 1, 8 : 8 + ROWS], 1, (la, west)),
    )
    up = send(st.at[:, 31:32], S.at[HALO:high, 7:8], 8, (la + 1, lo))
    down = send(st.at[:, 0:1], S.at[HALO:high, 40:41], 9, (la - 1, lo))
    up_east = send(st.at[last:COLS, 31:32], S.at[0:HALO, 7:8], 10, (la + 1, east))
    up_west = send(st.at[0:HALO, 31:32], S.at[high : high + HALO, 7:8], 11, (la + 1, west))
    down_east = send(st.at[last:COLS, 0:1], S.at[0:HALO, 40:41], 12, (la - 1, east))
    down_west = send(st.at[0:HALO, 0:1], S.at[high : high + HALO, 40:41], 13, (la - 1, west))

    def start(*copies):
        for copy in copies:
            copy.start()

    def wait_send(*copies):
        for copy in copies:
            copy.wait_send()

    def wait_recv(*copies):
        for copy in copies:
            copy.wait_recv()

    to_up = has_up & is_polar(la + 1)
    to_down = has_down & is_polar(la - 1)

    def start_east_far():
        pl.when(to_up)(lambda: start(up_east))
        pl.when(to_down)(lambda: start(down_east))

    def start_east():
        pl.when(polar)(lambda: start(wide[0]))
        pl.when(jnp.logical_not(polar))(lambda: start(thin[0]))

    def start_west_far():
        pl.when(to_up)(lambda: start(up_west))
        pl.when(to_down)(lambda: start(down_west))

    def start_west():
        pl.when(polar)(lambda: start(wide[1]))
        pl.when(jnp.logical_not(polar))(lambda: start(thin[1]))

    def start_lat():
        pl.when(has_up)(lambda: start(up))
        pl.when(has_down)(lambda: start(down))

    @pl.when(final)
    def _():
        tell_one(from_west, (la, east))
        swift = la == 1
        pl.when(jnp.logical_not(swift))(start_east_far)
        late = (lo == 15) & ((la == 0) | (la == 3))
        pl.when(jnp.logical_not(late))(start_east)
        pl.when(swift)(start_east_far)
        tell(barrier, west)
        pl.when(late)(start_east)

    pl.when(even & jnp.logical_not(final))(lambda: tell_lat(from_lat))

    @pl.when(inside)
    def _():
        tell(from_east, west)

        @pl.when(pivot)
        def _():
            tell_one(from_west, (la, east))
            tell_far(from_far, east)

    pl.when(even & jnp.logical_not(final))(start_lat)
    pl.when(inside)(start_west_far)
    pl.when(inside)(start_west)
    pl.when(pivot)(start_east_far)
    pl.when(pivot)(start_east)
    pl.when(jnp.logical_not(first))(fetch)

    prepare()
    body.wait()

    pl.when(polar & first)(lambda: inner(1))

    @pl.when(odd & jnp.logical_not(final))
    def _():
        pl.semaphore_wait(from_lat, beside)
        start_lat()

    @pl.when(rising)
    def _():
        pl.semaphore_wait(from_east, neighbours)
        start_east_far()
        start_east()

    @pl.when(final)
    def _():
        pl.semaphore_wait(from_west, 1)
        start_lat()
        pl.semaphore_wait(from_far, beside)
        start_west_far()
        start_west()

    def answer():
        pl.semaphore_wait(from_west, 1)
        tell_lat(from_far)
        start_west()

    def answer_far():
        pl.semaphore_wait(from_far, beside)
        start_west_far()

    def clear(row):
        S[:, row : row + 1, :] = jnp.zeros((S.shape[0], 1, CH), F32)

    pl.when(jnp.logical_not(has_down))(lambda: clear(7))
    pl.when(jnp.logical_not(has_up))(lambda: clear(40))

    pl.when(polar & jnp.logical_not(first))(lambda: inner(1))
    pl.when(lo == 8)(answer)
    pl.when(polar)(lambda: inner(2))
    pl.when((lo == 0) & jnp.logical_not(polar))(answer)
    pl.when(has_down)(lambda: wait_recv(up))
    pl.when(has_up)(lambda: wait_recv(down))

    @pl.when(polar)
    def _():
        inner(0)
        pl.when(lo == 0)(answer)
        pl.when(lo == 8)(answer_far)
        inner(3)
        both_edges(True)

        pl.when(lo == 0)(answer_far)
        arrive(True)
        arrive(False)

    @pl.when(jnp.logical_not(polar))
    def _():
        wait_recv(*thin)
        for t in range(TILES):
            plain(t)
        pl.when(first)(answer_far)

    pl.when(polar)(lambda: wait_send(*wide))
    pl.when(jnp.logical_not(polar))(lambda: wait_send(*thin))
    pl.when(has_up)(lambda: wait_send(up))
    pl.when(has_down)(lambda: wait_send(down))
    pl.when(to_up)(lambda: wait_send(up_east, up_west))
    pl.when(to_down)(lambda: wait_send(down_east, down_west))


def local(
    state, zonal_coef, diffusivity, coupling, filter_rows, band_width, table_index, coef_table
):
    turned = jnp.transpose(state, (1, 0, 2))
    args = (
        turned, zonal_coef[None, :], diffusivity[None, :], coupling,
        filter_rows[None, :], band_width[None, :], table_index[None, :], coef_table,
    )
    vmem = pl.BlockSpec(memory_space=pltpu.VMEM)
    parts = pl.pallas_call(
        kernel,
        out_shape=(
            pltpu.VMEM((COLS, ROWS, CH), F32),
            pltpu.VMEM((COLS + 2 * HALO, ROWS + 16, CH), F32),
            pltpu.VMEM((MAXB + 1, TILES, 8, CH), F32),
            pltpu.VMEM((ROWS, CH), F32),
            pltpu.VMEM((ROWS, CH), F32),
            pltpu.VMEM((2 * CH, 2 * CH), BF16),
            pltpu.VMEM((1, CH), F32),
        ),
        in_specs=[pl.BlockSpec(memory_space=pltpu.HBM)] * len(args),
        out_specs=(vmem,) * 7,
        scratch_shapes=[pltpu.VMEM((TILES, COLS + 2 * MAXB, 8, CH), F32)]
        + [pltpu.VMEM(args[i].shape, args[i].dtype) for i in (1, 3, 4, 5, 6, 7)]
        + [
            pltpu.SemaphoreType.DMA((14,)),
            pltpu.SemaphoreType.DMA((14,)),
            pltpu.SemaphoreType.DMA((8,)),
            pltpu.SemaphoreType.REGULAR,
            pltpu.SemaphoreType.REGULAR,
            pltpu.SemaphoreType.REGULAR,
            pltpu.SemaphoreType.REGULAR,
        ],
        compiler_params=pltpu.CompilerParams(
            collective_id=0, has_side_effects=True, vmem_limit_bytes=53 * 1024 * 1024
        ),
    )(*args)
    updated = pl.pallas_call(
        finish,
        out_shape=pltpu.HBM((COLS, ROWS, CH), F32),
        in_specs=[vmem] * 7,
        out_specs=pl.BlockSpec(memory_space=pltpu.HBM),
        scratch_shapes=[
            pltpu.VMEM((TILES, 2 * HALO, 8, CH), F32),
            pltpu.VMEM((2 * HALO, ROWS, CH), F32),
            pltpu.SemaphoreType.DMA((3,)),
        ],
        compiler_params=pltpu.CompilerParams(vmem_limit_bytes=32 * 1024 * 1024),
    )(*parts)
    return jnp.transpose(updated, (1, 0, 2))


def solution(mesh):
    return jax.shard_map(
        local,
        mesh=mesh,
        in_specs=(P("lat", "lon", None), P("lat"), P(), P(), P(), P(), P(), P()),
        out_specs=P("lat", "lon", None),
        check_vma=False,
    )
```
